256 devices in a mesh: row: 32 (over z, y), col: 8 (over x, core).
Axes of the slice: x: 4, y: 4, z: 8, core: 2. Of those that a mesh axis runs over, the one named last changes fastest.
Arguments:
- coupling: float32 [1, 8, 4, 32, 512, 512], P(None, 'col', None, 'row'), may hold values from -0.046875 to 0.046875
- earlier: float32 [4, 32, 512, 1536], P(None, 'row'), may hold values from -6 to 6
- right_sides: float32 [1, 8, 512, 1536], P(None, 'col', 'row'), may hold values from -6 to 6
- panel_blocks: float32 [1, 8, 2, 512, 512], P(None, 'col', None, 'row'), may hold values from -4 to 4, as said below
- block_inverses: float32 [2, 512, 512], replicated, may hold values from -4 to 4, as said below
Outputs:
- solved: float32 [2, 512, 1536], replicated
- pending: float32 [1, 8, 512, 1536], P(None, 'col', 'row')
The draws below stay inside these ranges and needn't reach their ends.
Inputs may be any that keep to these rules, and one draw needn't show every extreme that they name: `panel_blocks`: block row a * 8 + c of column index k is zero where a * 8 + c >= 7 - k. `block_inverses`: each block is upper triangular with a positive diagonal.
All inputs are finite; a program needn't handle non-finite values.
Results may differ from the reference program's by a relative error of at most 0.000088.
Values sent between devices are 32-bit elements; how exact they have to be, the bound alone decides.
No kernel may reach another device: no remote copies, remote signals or barrier semaphores. Data moves between devices by JAX's collectives and lax.ppermute only.
A program may use at most 128 MiB of HBM per device.

```python
import jax
import jax.numpy as jnp
from jax import lax

NB = 512
SAMPLES = 1536
CB = 4
RB = 1
KC = 128
N_ROW = 32
N_COL = 8


def draw_panel_blocks(key, part):
    key = jax.random.fold_in(key, 11)
    shape = (RB, N_COL, 2, NB, NB)
    values = jnp.clip(jax.random.normal(key, shape, jnp.float32), -4.0, 4.0)
    values = values * NB ** (-0.5)
    block_row = lax.broadcasted_iota(jnp.int32, shape, 0) * N_COL + lax.broadcasted_iota(jnp.int32, shape, 1)
    column = lax.broadcasted_iota(jnp.int32, shape, 2)
    keep = block_row < RB * N_COL - 1 - column
    return jnp.where(keep, values, jnp.zeros_like(values))


def draw_block_inverses(key, part):
    key = jax.random.fold_in(key, 23)
    key_off, key_diag = jax.random.split(key)
    shape = (2, NB, NB)
    off_part = jnp.clip(jax.random.normal(key_off, shape, jnp.float32), -4.0, 4.0)
    off_part = off_part * NB ** (-0.5)
    diag_part = jnp.exp(jax.random.uniform(key_diag, shape, jnp.float32, -0.69, 0.69))
    rows = lax.broadcasted_iota(jnp.int32, shape, 1)
    cols = lax.broadcasted_iota(jnp.int32, shape, 2)
    return jnp.where(rows < cols, off_part, jnp.where(rows == cols, diag_part, jnp.zeros_like(off_part)))


def raised(result, stream_key, source, target, shards_of, factor):
    owner, partner = [(jnp.arange(result.shape[position]) // (result.shape[position] // shards_of)).reshape([-1 if axis == position else 1 for axis in range(result.ndim)]) for position in (source, target)]
    chosen = jax.random.permutation(stream_key, shards_of)[partner]
    strong = (owner == chosen) | (owner == (partner + shards_of // 2) % shards_of)
    return jnp.where(strong, factor * result, result)


def steps_of(stream_key, shape, cuts, smallest, top_value):
    factor_of, own = 1.0, jax.random.fold_in(stream_key, 6)
    for position, shards_of in cuts:
        heights = jnp.exp(jax.random.uniform(jax.random.fold_in(own, position), (shards_of,), jnp.float32, smallest / len(cuts), top_value / len(cuts)))
        factor_of = factor_of * jnp.repeat(heights, shape[position] // shards_of).reshape([-1 if axis == position else 1 for axis in range(len(shape))])
    return factor_of


def noise(key, extent, scale, most, shards=(), kind=jnp.bfloat16):
    array = jax.random.normal(key, extent, jnp.float32) * scale
    if len(shards) > 0:
        array = steps_of(key, extent, shards, -0.22, 0.18) * array
    return jnp.clip(array, min=-most, max=most).astype(kind)


def bell_draw_with(rng, dims, scale, reach, cuts, heavy, kind=jnp.bfloat16):
    result = scale * jax.random.normal(rng, dims, jnp.float32)
    if cuts:
        result = result * steps_of(rng, dims, cuts, -0.22, 0.18)
    return jnp.clip(raised(result, jax.random.fold_in(rng, 3), *heavy), -reach, reach).astype(kind)


def setup_inputs(seed: int = 0) -> dict:
    splits = jax.random.split(jax.random.key(seed), 6)
    coupling = bell_draw_with(splits[0], (RB, N_COL, CB, N_ROW, NB, NB), (KC * NB) ** -0.5, 0.046875, ((1, 8), (3, 32)), (3, 4, 32, 2.75), jnp.float32)
    earlier = noise(splits[1], (CB, N_ROW, NB, SAMPLES), 1.0, 6.0, ((1, 32),), jnp.float32)
    right_sides = noise(splits[2], (RB, N_COL, NB, SAMPLES), 1.0, 6.0, ((1, 8), (2, 32)), jnp.float32)
    panel_blocks = draw_panel_blocks(jax.random.fold_in(splits[5], 71), 0)
    block_inverses = draw_block_inverses(jax.random.fold_in(splits[5], 71), 0)
    return {"coupling": coupling, "earlier": earlier, "right_sides": right_sides, "panel_blocks": panel_blocks, "block_inverses": block_inverses}


def reference(coupling, earlier, right_sides, panel_blocks, block_inverses):
    hp = lax.Precision.HIGHEST
    update = jnp.einsum("acbrij,brjs->acis", coupling, earlier, precision=hp)
    base = right_sides - update
    first = jnp.dot(block_inverses[0], base[RB - 1, N_COL - 1], precision=hp, preferred_element_type=jnp.float32)
    middle = base - jnp.einsum("acij,js->acis", panel_blocks[:, :, 0], first, precision=hp)
    second = jnp.dot(block_inverses[1], middle[RB - 1, N_COL - 2], precision=hp, preferred_element_type=jnp.float32)
    pending = middle - jnp.einsum("acij,js->acis", panel_blocks[:, :, 1], second, precision=hp)
    return jnp.stack([first, second]), pending
```

```python
import functools

import jax
import jax.numpy as jnp
from jax import lax
from jax.experimental import pallas as pl
from jax.experimental.pallas import tpu as pltpu
from jax.sharding import Mesh
from jax.sharding import PartitionSpec as P

NZ, NY, NX, NCORE = 8, 4, 4, 2
SLAB = 16
HALF = 768
PART = 384
BITREV = (0, 4, 2, 6, 1, 5, 3, 7)
HALVES = (((0, 3, 1, 2), (1, 3), 0), ((0, 1, 3, 2), (3, 1), 1))


def split(x):
    high = x.astype(jnp.bfloat16)
    return high, (x - high.astype(jnp.float32)).astype(jnp.bfloat16)


def dot3(a, b):
    ah, al = split(a)
    bh, bl = split(b)
    mul = functools.partial(jnp.dot, preferred_element_type=jnp.float32)
    return mul(ah, bh) + (mul(ah, bl) + mul(al, bh))


def term_kernel(index_ref, c_ref, e_ref, o_ref, acc):
    k = pl.program_id(0)
    product = dot3(c_ref[0], e_ref[0])

    @pl.when(k == 0)
    def _():
        acc[...] = product

    @pl.when(k > 0)
    def _():
        acc[...] += product

    @pl.when(k == pl.num_programs(0) - 1)
    def _():
        for i in range(NZ * NY):
            row = pl.multiple_of(index_ref[i] * SLAB, SLAB)
            o_ref[i] = acc[pl.ds(row, SLAB), :]


def term(index, coupling, earlier, half):
    return pl.pallas_call(
        term_kernel,
        grid_spec=pltpu.PrefetchScalarGridSpec(
            num_scalar_prefetch=1,
            grid=(4,),
            in_specs=[
                pl.BlockSpec((1, 512, 512), lambda k, i: (k, 0, 0)),
                pl.BlockSpec((1, 512, HALF), lambda k, i: (k, 0, half)),
            ],
            out_specs=pl.BlockSpec((NZ * NY, SLAB, HALF), lambda k, i: (0, 0, 0)),
            scratch_shapes=[pltpu.VMEM((512, HALF), jnp.float32)],
        ),
        out_shape=jax.ShapeDtypeStruct((NZ * NY, SLAB, HALF), jnp.float32),
        compiler_params=pltpu.CompilerParams(vmem_limit_bytes=24 * 2**20),
        cost_estimate=pl.CostEstimate(
            flops=6 * 512 * 2048 * HALF, bytes_accessed=12 * 2**20, transcendentals=0
        ),
        name="term",
    )(index, coupling, earlier)


def solve_kernel(counts, index_ref, inv_ref, link_ref, *refs):
    pieces, o_ref, b = refs[: len(counts)], refs[len(counts)], refs[len(counts) + 1]
    at = 0
    for piece, count in zip(pieces, counts):
        for i in range(count):
            row = pl.multiple_of(index_ref[at] * SLAB, SLAB)
            b[:, pl.ds(row, SLAB), :] = piece[i]
            at += 1
    first = dot3(inv_ref[0], b[0])
    o_ref[0] = first
    middle = b[1] - dot3(link_ref[...], first)
    o_ref[1] = dot3(inv_ref[1], middle)


def solve(index, inverses, link, pieces):
    counts = tuple(p.shape[0] for p in pieces)
    whole = pl.BlockSpec(memory_space=pltpu.VMEM)
    return pl.pallas_call(
        functools.partial(solve_kernel, counts),
        in_specs=[pl.BlockSpec(memory_space=pltpu.SMEM)] + [whole] * (2 + len(pieces)),
        out_specs=whole,
        scratch_shapes=[pltpu.VMEM((2, 512, PART), jnp.float32)],
        out_shape=jax.ShapeDtypeStruct((2, 512, PART), jnp.float32),
        compiler_params=pltpu.CompilerParams(vmem_limit_bytes=24 * 2**20),
        cost_estimate=pl.CostEstimate(
            flops=18 * 512 * 512 * PART, bytes_accessed=6 * 2**20, transcendentals=0
        ),
        name="solve",
    )(index, inverses, link, *pieces)


def finish_kernel(core_ref, own1, own2, other1, other2, base_a, base_b, panel, solved, pending, sems):
    core = core_ref[0]
    mine, theirs = core * HALF, (1 - core) * HALF
    places = ((own1, mine), (own2, mine + PART), (other1, theirs), (other2, theirs + PART))
    copies = []
    for i, (ref, at) in enumerate(places):
        columns = pl.ds(pl.multiple_of(at, 128), PART)
        copies.append(pltpu.make_async_copy(ref, solved.at[:, :, columns], sems.at[i]))
        copies[-1].start()
    pending[:, :HALF] = base_a[...]
    pending[:, HALF:] = base_b[...]
    for ref, at in places:
        columns = pl.ds(pl.multiple_of(at, 128), PART)
        update = dot3(panel[0], ref[0]) + dot3(panel[1], ref[1])
        pending[:, columns] = pending[:, columns] - update
    for copy in copies:
        copy.wait()


def finish(core, own1, own2, other1, other2, base_a, base_b, panel):
    whole = pl.BlockSpec(memory_space=pltpu.VMEM)
    return pl.pallas_call(
        finish_kernel,
        in_specs=[pl.BlockSpec(memory_space=pltpu.SMEM)] + [whole] * 7,
        out_specs=(pl.BlockSpec(memory_space=pl.ANY), whole),
        scratch_shapes=[pltpu.SemaphoreType.DMA((4,))],
        out_shape=(
            jax.ShapeDtypeStruct((2, 512, 2 * HALF), jnp.float32),
            jax.ShapeDtypeStruct((SLAB, 2 * HALF), jnp.float32),
        ),
        compiler_params=pltpu.CompilerParams(vmem_limit_bytes=24 * 2**20),
        name="finish",
    )(core, own1, own2, other1, other2, base_a, base_b, panel)


def swap_y(x, bit):
    return lax.ppermute(x, "y", [(i, i ^ bit) for i in range(NY)])


def swap_z(x, bit, shift):
    pairs = [(i, ((((i + shift) % NZ) ^ bit) - shift) % NZ) for i in range(NZ)]
    return lax.ppermute(x, "z", pairs)


def swap_core(x):
    return lax.ppermute(x, "core", [(0, 1), (1, 0)])


def step(x, axis, by):
    n = lax.axis_size(axis)
    return lax.ppermute(x, axis, [(i, (i + by) % n) for i in range(n)])


def slab_index(z, y, half):
    order, _, shift = HALVES[half]
    label = (z + shift) % NZ
    rows = []
    for ky in order:
        for kz in BITREV:
            rows.append((((label ^ kz) - shift) % NZ) * NY + (y ^ ky))
    return jnp.stack(rows).astype(jnp.int32)


def reduce_half(slabs, half):
    _, (bit1, bit2), shift = HALVES[half]
    slabs = slabs[:16] + swap_y(slabs[16:], bit1)
    slabs = slabs[:8] + swap_y(slabs[8:], bit2)
    slabs = slabs[:4] + swap_z(slabs[4:], 1, shift)
    slabs = slabs[:2] + swap_z(slabs[2:], 2, shift)
    return slabs[0] + swap_z(slabs[1:], 4, shift)[0]


def gather_z(v):
    out, offsets = [v], [0]
    up = down = v
    for s in (1, 2, 3):
        up, down = step(up, "z", 1), step(down, "z", -1)
        out += [up, down]
        offsets += [-s, s]
    h = v.shape[0] // 2
    out += [step(up[:h], "z", 1), step(down[h:], "z", -1)]
    offsets += [4, 4]
    return out, offsets


def gather_y(v):
    up, down = step(v, "y", 1), step(v, "y", -1)
    h = v.shape[0] // 2
    return [v, up, down, step(up[:h], "y", 1), step(down[h:], "y", -1)], [0, -1, 1, 2, 2]


def local(coupling, earlier, right_sides, panel_blocks, block_inverses):
    z, y, x, core = (lax.axis_index(a) for a in ("z", "y", "x", "core"))
    coupling, earlier = coupling[0, 0, :, 0], earlier[:, 0]
    right, panel = right_sides[0, 0], panel_blocks[0, 0]

    link = lax.all_gather(panel[0], ("x", "core"), axis=0)[6]
    link = lax.all_gather(link, ("z", "y"), axis=0, tiled=True)

    base = []
    for half in (0, 1):
        slabs = term(slab_index(z, y, half), coupling, earlier, half)
        total = reduce_half(slabs, half)
        base.append(right[:, half * HALF : (half + 1) * HALF] - total)
    base_a, base_b = base

    is_first = core == 0
    kept = jnp.where(is_first, base_a, base_b)
    came = swap_core(jnp.where(is_first, base_b, base_a))
    v = jnp.stack([jnp.where(is_first, came, kept), jnp.where(is_first, kept, came)])
    others = [lax.ppermute(v, "x", [(NX - 1, i)]) for i in range(NX - 1)]
    v = jnp.where(x == NX - 1, v, others[0] + others[1] + others[2])

    v1 = v[:, :, :PART]
    blocks, offs = gather_z(v1)
    far = jnp.concatenate(blocks[7:])
    blocks, offs = blocks[:7] + [far], offs[:8]
    pieces1, y_offs = gather_y(jnp.stack(blocks))
    index1 = []
    for i, (piece, oy) in enumerate(zip(pieces1, y_offs)):
        zs = offs if i < 3 else (offs[:4] if i == 3 else offs[4:])
        index1 += [((z + oz) % NZ) * NY + (y + oy) % NY for oz in zs]
    v2 = v[:, :, PART:]
    blocks, offs = gather_y(v2)
    far = jnp.concatenate(blocks[3:])
    blocks, offs = blocks[:3] + [far], offs[:4]
    pieces2, z_offs = gather_z(jnp.stack(blocks))
    index2 = []
    for i, (piece, oz) in enumerate(zip(pieces2, z_offs)):
        ys = offs if i < 7 else (offs[:2] if i == 7 else offs[2:])
        index2 += [((z + oz) % NZ) * NY + (y + oy) % NY for oy in ys]

    own1 = solve(jnp.stack(index1).astype(jnp.int32), block_inverses, link, pieces1)
    own2 = solve(jnp.stack(index2).astype(jnp.int32), block_inverses, link, pieces2)
    other1, other2 = swap_core(own1), swap_core(own2)
    core = core.astype(jnp.int32).reshape(1)
    solved, pending = finish(core, own1, own2, other1, other2, base_a, base_b, panel)
    return solved, pending[None, None]


def solution(mesh):
    inner = Mesh(mesh.devices.reshape(NZ, NY, NX, NCORE), ("z", "y", "x", "core"))
    row, col = ("z", "y"), ("x", "core")
    in_specs = (
        P(None, col, None, row, None, None),
        P(None, row, None, None),
        P(None, col, row, None),
        P(None, col, None, row, None),
        P(),
    )
    out_specs = (P(), P(None, col, row, None))
    return jax.shard_map(local, mesh=inner, in_specs=in_specs, out_specs=out_specs, check_vma=False)
```

```python
import functools

import jax
import jax.numpy as jnp
from jax import lax
from jax.experimental import pallas as pl
from jax.experimental.pallas import tpu as pltpu
from jax.sharding import Mesh
from jax.sharding import PartitionSpec as P

NZ, NY, NX, NCORE = 8, 4, 4, 2
SLAB = 16
HALF = 768
PART = 384
BITREV = (0, 4, 2, 6, 1, 5, 3, 7)
HALVES = (((0, 3, 1, 2), (1, 3)), ((0, 1, 3, 2), (3, 1)))


def split(x):
    high = x.astype(jnp.bfloat16)
    return high, (x - high.astype(jnp.float32)).astype(jnp.bfloat16)


def dot3(a, b):
    ah, al = split(a)
    bh, bl = split(b)
    mul = functools.partial(jnp.dot, preferred_element_type=jnp.float32)
    return mul(ah, bh) + (mul(ah, bl) + mul(al, bh))


def term_kernel(index_ref, c_ref, ea_ref, eb_ref, oa_ref, ob_ref, acc):
    k = pl.program_id(0)
    product = dot3(c_ref[0], jnp.concatenate([ea_ref[0], eb_ref[0]], axis=1))

    @pl.when(k == 0)
    def _():
        acc[...] = product

    @pl.when(k > 0)
    def _():
        acc[...] += product

    @pl.when(k == pl.num_programs(0) - 1)
    def _():
        for half, o_ref in enumerate((oa_ref, ob_ref)):
            for i in range(NZ * NY):
                row = pl.multiple_of(index_ref[half * NZ * NY + i] * SLAB, SLAB)
                o_ref[i] = acc[pl.ds(row, SLAB), half * PART : (half + 1) * PART]


def term(index, coupling, earlier, chunk):
    out = pl.BlockSpec((NZ * NY, SLAB, PART), lambda k, i: (0, 0, 0))
    return pl.pallas_call(
        term_kernel,
        grid_spec=pltpu.PrefetchScalarGridSpec(
            num_scalar_prefetch=1,
            grid=(4,),
            in_specs=[
                pl.BlockSpec((1, 512, 512), lambda k, i: (k, 0, 0)),
                pl.BlockSpec((1, 512, PART), lambda k, i: (k, 0, chunk)),
                pl.BlockSpec((1, 512, PART), lambda k, i: (k, 0, 2 + chunk)),
            ],
            out_specs=(out, out),
            scratch_shapes=[pltpu.VMEM((512, HALF), jnp.float32)],
        ),
        out_shape=(jax.ShapeDtypeStruct((NZ * NY, SLAB, PART), jnp.float32),) * 2,
        compiler_params=pltpu.CompilerParams(vmem_limit_bytes=56 * 2**20),
        cost_estimate=pl.CostEstimate(
            flops=6 * 512 * 2048 * HALF, bytes_accessed=12 * 2**20, transcendentals=0
        ),
        name="term",
    )(index, coupling, earlier, earlier)


def solve_kernel(counts, with_link, index_ref, core_ref, inv_ref, *refs):
    pieces, refs = refs[: len(counts)], refs[len(counts) :]
    if with_link:
        link_own, link_other, o_ref, link_ref, b = refs
    else:
        link_ref, o_ref, b = refs
    rows, at = [], 0
    for piece, count in zip(pieces, counts):
        for i in range(count):
            rows.append(pl.ds(pl.multiple_of(index_ref[at] * SLAB, SLAB), SLAB))
            for block in (0, 1):
                b[block, rows[at], :] = piece[i, :, block * PART : (block + 1) * PART]
            at += 1
    if with_link:
        here = pl.ds(pl.multiple_of(core_ref[0] * 256, 128), 256)
        there = pl.ds(pl.multiple_of((1 - core_ref[0]) * 256, 128), 256)
        for i, row in enumerate(rows):
            link_ref[row, here] = link_own[i]
            link_ref[row, there] = link_other[i]
    first = dot3(inv_ref[0], b[0])
    o_ref[0] = first
    middle = b[1] - dot3(link_ref[...], first)
    o_ref[1] = dot3(inv_ref[1], middle)


def solve(index, core, inverses, pieces, links):
    counts = tuple(p.shape[0] for p in pieces)
    with_link = len(links) == 2
    whole = pl.BlockSpec(memory_space=pltpu.VMEM)
    scalar = pl.BlockSpec(memory_space=pltpu.SMEM)
    out = jax.ShapeDtypeStruct((2, 512, PART), jnp.float32)
    link = jax.ShapeDtypeStruct((512, 512), jnp.float32)
    return pl.pallas_call(
        functools.partial(solve_kernel, counts, with_link),
        in_specs=[scalar] * 2 + [whole] * (1 + len(pieces) + len(links)),
        out_specs=(whole, whole) if with_link else whole,
        scratch_shapes=[pltpu.VMEM((2, 512, PART), jnp.float32)],
        out_shape=(out, link) if with_link else out,
        compiler_params=pltpu.CompilerParams(vmem_limit_bytes=24 * 2**20),
        cost_estimate=pl.CostEstimate(
            flops=18 * 512 * 512 * PART, bytes_accessed=6 * 2**20, transcendentals=0
        ),
        name="solve",
    )(index, core, inverses, *pieces, *links)


def finish_kernel(core_ref, own1, own2, other1, other2, a1, b1, a2, b2, panel, solved, pending, sems):
    core = core_ref[0]
    mine, theirs = core * HALF, (1 - core) * HALF
    places = ((own1, mine), (own2, mine + PART), (other1, theirs), (other2, theirs + PART))
    copies = []
    for i, (ref, at) in enumerate(places):
        columns = pl.ds(pl.multiple_of(at, 128), PART)
        copies.append(pltpu.make_async_copy(ref, solved.at[:, :, columns], sems.at[i]))
        copies[-1].start()
    for i, base in enumerate((a1, a2, b1, b2)):
        pending[:, i * PART : (i + 1) * PART] = base[...]
    for ref, at in places:
        columns = pl.ds(pl.multiple_of(at, 128), PART)
        update = dot3(panel[0], ref[0]) + dot3(panel[1], ref[1])
        pending[:, columns] = pending[:, columns] - update
    for copy in copies:
        copy.wait()


def finish(core, *operands):
    whole = pl.BlockSpec(memory_space=pltpu.VMEM)
    return pl.pallas_call(
        finish_kernel,
        in_specs=[pl.BlockSpec(memory_space=pltpu.SMEM)] + [whole] * len(operands),
        out_specs=(pl.BlockSpec(memory_space=pl.ANY), whole),
        scratch_shapes=[pltpu.SemaphoreType.DMA((4,))],
        out_shape=(
            jax.ShapeDtypeStruct((2, 512, 2 * HALF), jnp.float32),
            jax.ShapeDtypeStruct((SLAB, 2 * HALF), jnp.float32),
        ),
        compiler_params=pltpu.CompilerParams(vmem_limit_bytes=24 * 2**20),
        name="finish",
    )(core, *operands)


def swap(x, axis, bit):
    return lax.ppermute(x, axis, [(i, i ^ bit) for i in range(lax.axis_size(axis))])


def step(x, axis, by):
    n = lax.axis_size(axis)
    return lax.ppermute(x, axis, [(i, (i + by) % n) for i in range(n)])


def reduce_rows(slabs):
    near = []
    for half in (0, 1):
        first, second = HALVES[half][1]
        s = slabs[half]
        s = s[:16] + swap(s[16:], "y", first)
        near.append(s[:8] + swap(s[8:], "y", second))
    s = jnp.stack(near, axis=1)
    s = s[:4] + swap(s[4:], "z", 1)
    s = s[:2] + swap(s[2:], "z", 2)
    s = s[:1] + swap(s[1:], "z", 4)
    return s[0, 0], s[0, 1]


def spread_x(v):
    others = [lax.ppermute(v, "x", [(NX - 1, i)]) for i in range(NX - 1)]
    return jnp.where(lax.axis_index("x") == NX - 1, v, others[0] + others[1] + others[2])


def gather_rows(v):
    v = v[None]
    for bit in (4, 2, 1):
        v = jnp.concatenate([v, swap(v, "z", bit)])
    up, down = step(v, "y", 1), step(v, "y", -1)
    return [v, up, down, step(up[:4], "y", 1), step(down[4:], "y", -1)]


def local(coupling, earlier, right_sides, panel_blocks, block_inverses):
    z, y, core = (lax.axis_index(a) for a in ("z", "y", "core"))
    coupling, earlier = coupling[0, 0, :, 0], earlier[:, 0]
    right, panel = right_sides[0, 0], panel_blocks[0, 0]
    is_first = core == 0
    core_id = core.astype(jnp.int32).reshape(1)

    slab_order = [(z ^ kz) * NY + (y ^ ky) for order, _ in HALVES for ky in order for kz in BITREV]
    slab_order = jnp.stack(slab_order).astype(jnp.int32)
    offsets = ((0, BITREV), (-1, BITREV), (1, BITREV), (2, BITREV[:4]), (2, BITREV[4:]))
    row_order = [(z ^ kz) * NY + (y + oy) % NY for oy, along in offsets for kz in along]
    row_order = jnp.stack(row_order).astype(jnp.int32)

    bases, solutions = [], []
    link = None
    for chunk in (0, 1):
        slabs = term(slab_order, coupling, earlier, chunk)
        if chunk == 0:
            slabs, coupling = lax.optimization_barrier((slabs, coupling))
        total = reduce_rows(slabs)
        at = chunk * PART
        base = right[:, at : at + PART] - total[0], right[:, HALF + at : HALF + at + PART] - total[1]
        bases += base
        kept = jnp.where(is_first, base[0], base[1])
        given = jnp.where(is_first, base[1], base[0])
        if chunk == 0:
            given = jnp.concatenate([given, panel[0, :, 256:]], axis=1)
        came = swap(given, "core", 1)
        last = jnp.where(is_first, came[:, :PART], kept)
        other = jnp.where(is_first, kept, came[:, :PART])
        v = [last, other]
        if chunk == 0:
            v.append(jnp.where(is_first, panel[0, :, :256], came[:, PART:]))
        pieces = gather_rows(spread_x(jnp.concatenate(v, axis=1)))
        if chunk == 0:
            part = jnp.concatenate([p[:, :, HALF:] for p in pieces])
            own, link = solve(row_order, core_id, block_inverses, pieces, (part, swap(part, "core", 1)))
        else:
            own = solve(row_order, core_id, block_inverses, pieces, (link,))
        solutions.append((own, swap(own, "core", 1)))
    (own1, other1), (own2, other2) = solutions
    solved, pending = finish(core_id, own1, own2, other1, other2, *bases, panel)
    return solved, pending[None, None]


def solution(mesh):
    inner = Mesh(mesh.devices.reshape(NZ, NY, NX, NCORE), ("z", "y", "x", "core"))
    row, col = ("z", "y"), ("x", "core")
    in_specs = (
        P(None, col, None, row, None, None),
        P(None, row, None, None),
        P(None, col, row, None),
        P(None, col, None, row, None),
        P(),
    )
    out_specs = (P(), P(None, col, row, None))
    return jax.shard_map(local, mesh=inner, in_specs=in_specs, out_specs=out_specs, check_vma=False)
```

```python
import functools

import jax
import jax.numpy as jnp
from jax import lax
from jax.experimental import pallas as pl
from jax.experimental.pallas import tpu as pltpu
from jax.sharding import Mesh
from jax.sharding import PartitionSpec as P

NZ, NY, NX, NCORE = 8, 4, 4, 2
SLAB = 16
HALF = 768
PART = 384
def split(x):
    high = x.astype(jnp.bfloat16)
    return high, (x - high.astype(jnp.float32)).astype(jnp.bfloat16)


def dot3(a, b):
    ah, al = split(a)
    bh, bl = split(b)
    mul = functools.partial(jnp.dot, preferred_element_type=jnp.float32)
    return mul(ah, bh) + (mul(ah, bl) + mul(al, bh))


def term_kernel(y_ref, c_ref, ea_ref, eb_ref, *refs):
    outs, acc = refs[:NY], refs[NY]
    k = pl.program_id(0)
    product = dot3(c_ref[0], jnp.concatenate([ea_ref[0], eb_ref[0]], axis=1))

    @pl.when(k == 0)
    def _():
        acc[...] = product

    @pl.when(k > 0)
    def _():
        acc[...] += product

    @pl.when(k == pl.num_programs(0) - 1)
    def _():
        for ky, o_ref in enumerate(outs):
            for z in range(NZ):
                row = pl.multiple_of((z * NY + (y_ref[0] ^ ky)) * SLAB, SLAB)
                o_ref[z] = acc[pl.ds(row, SLAB), :]


def term(y, coupling, earlier, chunk):
    out = pl.BlockSpec((NZ, SLAB, HALF), lambda k, i: (0, 0, 0))
    return pl.pallas_call(
        term_kernel,
        grid_spec=pltpu.PrefetchScalarGridSpec(
            num_scalar_prefetch=1,
            grid=(4,),
            in_specs=[
                pl.BlockSpec((1, 512, 512), lambda k, i: (k, 0, 0)),
                pl.BlockSpec((1, 512, PART), lambda k, i: (k, 0, chunk)),
                pl.BlockSpec((1, 512, PART), lambda k, i: (k, 0, 2 + chunk)),
            ],
            out_specs=(out,) * NY,
            scratch_shapes=[pltpu.VMEM((512, HALF), jnp.float32)],
        ),
        out_shape=(jax.ShapeDtypeStruct((NZ, SLAB, HALF), jnp.float32),) * NY,
        compiler_params=pltpu.CompilerParams(vmem_limit_bytes=56 * 2**20),
        cost_estimate=pl.CostEstimate(
            flops=6 * 512 * 2048 * HALF, bytes_accessed=12 * 2**20, transcendentals=0
        ),
        name="term",
    )(y, coupling, earlier, earlier)


def solve_kernel(counts, with_link, index_ref, core_ref, inv_ref, *refs):
    pieces, refs = refs[: len(counts)], refs[len(counts) :]
    if with_link:
        link_own, link_other, o_ref, link_ref, b = refs
    else:
        link_ref, o_ref, b = refs
    rows, at = [], 0
    for piece, count in zip(pieces, counts):
        for i in range(count):
            rows.append(pl.ds(pl.multiple_of(index_ref[at] * SLAB, SLAB), SLAB))
            for block in (0, 1):
                b[block, rows[at], :] = piece[i, :, block * PART : (block + 1) * PART]
            at += 1
    if with_link:
        here = pl.ds(pl.multiple_of(core_ref[0] * 256, 128), 256)
        there = pl.ds(pl.multiple_of((1 - core_ref[0]) * 256, 128), 256)
        for i, row in enumerate(rows):
            link_ref[row, here] = link_own[i]
            link_ref[row, there] = link_other[i]
    first = dot3(inv_ref[0], b[0])
    o_ref[0] = first
    middle = b[1] - dot3(link_ref[...], first)
    o_ref[1] = dot3(inv_ref[1], middle)


def solve(index, core, inverses, pieces, links):
    counts = tuple(p.shape[0] for p in pieces)
    with_link = len(links) == 2
    whole = pl.BlockSpec(memory_space=pltpu.VMEM)
    scalar = pl.BlockSpec(memory_space=pltpu.SMEM)
    out = jax.ShapeDtypeStruct((2, 512, PART), jnp.float32)
    link = jax.ShapeDtypeStruct((512, 512), jnp.float32)
    return pl.pallas_call(
        functools.partial(solve_kernel, counts, with_link),
        in_specs=[scalar] * 2 + [whole] * (1 + len(pieces) + len(links)),
        out_specs=(whole, whole) if with_link else whole,
        scratch_shapes=[pltpu.VMEM((2, 512, PART), jnp.float32)],
        out_shape=(out, link) if with_link else out,
        compiler_params=pltpu.CompilerParams(vmem_limit_bytes=24 * 2**20),
        cost_estimate=pl.CostEstimate(
            flops=18 * 512 * 512 * PART, bytes_accessed=6 * 2**20, transcendentals=0
        ),
        name="solve",
    )(index, core, inverses, *pieces, *links)


def finish_kernel(core_ref, own1, own2, other1, other2, a1, b1, a2, b2, panel, solved, pending, sems):
    core = core_ref[0]
    mine, theirs = core * HALF, (1 - core) * HALF
    places = ((own1, mine), (own2, mine + PART), (other1, theirs), (other2, theirs + PART))
    copies = []
    for i, (ref, at) in enumerate(places):
        columns = pl.ds(pl.multiple_of(at, 128), PART)
        copies.append(pltpu.make_async_copy(ref, solved.at[:, :, columns], sems.at[i]))
        copies[-1].start()
    for i, base in enumerate((a1, a2, b1, b2)):
        pending[:, i * PART : (i + 1) * PART] = base[...]
    for ref, at in places:
        columns = pl.ds(pl.multiple_of(at, 128), PART)
        update = dot3(panel[0], ref[0]) + dot3(panel[1], ref[1])
        pending[:, columns] = pending[:, columns] - update
    for copy in copies:
        copy.wait()


def finish(core, *operands):
    whole = pl.BlockSpec(memory_space=pltpu.VMEM)
    return pl.pallas_call(
        finish_kernel,
        in_specs=[pl.BlockSpec(memory_space=pltpu.SMEM)] + [whole] * len(operands),
        out_specs=(pl.BlockSpec(memory_space=pl.ANY), whole),
        scratch_shapes=[pltpu.SemaphoreType.DMA((4,))],
        out_shape=(
            jax.ShapeDtypeStruct((2, 512, 2 * HALF), jnp.float32),
            jax.ShapeDtypeStruct((SLAB, 2 * HALF), jnp.float32),
        ),
        compiler_params=pltpu.CompilerParams(vmem_limit_bytes=24 * 2**20),
        name="finish",
    )(core, *operands)


def swap(x, axis, bit):
    return lax.ppermute(x, axis, [(i, i ^ bit) for i in range(lax.axis_size(axis))])


def step(x, axis, by):
    n = lax.axis_size(axis)
    return lax.ppermute(x, axis, [(i, (i + by) % n) for i in range(n)])


def after(x, *others):
    return lax.optimization_barrier((x, *others))[0]


def sum_y(slabs):
    near = slabs[0]
    for ky in range(1, NY):
        near = near + swap(slabs[ky], "y", ky)
    return near


def sum_z(near):
    return jnp.sum(lax.all_to_all(near, "z", 0, 0, tiled=True), axis=0)


def spread_x(v):
    others = [lax.ppermute(v, "x", [(NX - 1, i)]) for i in range(NX - 1)]
    return jnp.where(lax.axis_index("x") == NX - 1, v, others[0] + others[1] + others[2])


def gather_z(v):
    return lax.all_to_all(jnp.broadcast_to(v, (NZ, *v.shape)), "z", 0, 0, tiled=True)


def gather_y_once(v):
    return [v] + [swap(v, "y", ky) for ky in range(1, NY)]


def gather_y_twice(v):
    up, down = step(v, "y", 1), step(v, "y", -1)
    h = v.shape[0] // 2
    return [v, up, down, step(up[:h], "y", 1), step(down[h:], "y", -1)]


def local(coupling, earlier, right_sides, panel_blocks, block_inverses):
    y, core = lax.axis_index("y"), lax.axis_index("core")
    coupling, earlier = coupling[0, 0, :, 0], earlier[:, 0]
    right, panel = right_sides[0, 0], panel_blocks[0, 0]
    is_first = core == 0
    core_id = core.astype(jnp.int32).reshape(1)
    y_id = y.astype(jnp.int32).reshape(1)
    order_a = [z * NY + (y ^ ky) for ky in range(NY) for z in range(NZ)]
    order_b = [z * NY + (y + oy) % NY for oy in (0, -1, 1, 2) for z in range(NZ)]
    order_a, order_b = (jnp.stack(order).astype(jnp.int32) for order in (order_a, order_b))

    def halves(total, chunk):
        at = chunk * PART
        return (
            right[:, at : at + PART] - total[:, :PART],
            right[:, HALF + at : HALF + at + PART] - total[:, PART:],
        )

    def exchange(base, extra):
        kept = jnp.where(is_first, base[0], base[1])
        given = jnp.where(is_first, base[1], base[0])
        if extra is not None:
            given = jnp.concatenate([given, extra[:, 256:]], axis=1)
        came = swap(given, "core", 1)
        last = jnp.where(is_first, came[:, :PART], kept)
        other = jnp.where(is_first, kept, came[:, :PART])
        v = [last, other]
        if extra is not None:
            v.append(jnp.where(is_first, extra[:, :256], came[:, PART:]))
        return jnp.concatenate(v, axis=1)

    slabs_a = term(y_id, coupling, earlier, 0)
    slabs_b = term(y_id, after(coupling, *slabs_a), earlier, 1)
    base_a = halves(sum_z(sum_y(slabs_a)), 0)
    v_a = exchange(base_a, panel[0])
    base_b = halves(sum_z(after(sum_y(slabs_b), v_a)), 1)
    v_a = gather_z(after(spread_x(v_a), *base_b))
    v_b = exchange(tuple(after(part, v_a) for part in base_b), None)
    v_b = gather_z(spread_x(v_b))
    pieces_a = [after(p, v_b) for p in gather_y_once(v_a)]
    pieces_b = gather_y_twice(v_b)

    part = jnp.concatenate([p[:, :, HALF:] for p in pieces_a])
    part = after(part, *pieces_b[1:3])
    links = part, swap(part, "core", 1)
    own_a, link = solve(order_a, core_id, block_inverses, pieces_a, links)
    other_a = swap(own_a, "core", 1)
    own_b = solve(order_b, core_id, block_inverses, pieces_b, (after(link, other_a),))
    other_b = swap(own_b, "core", 1)
    solved, pending = finish(core_id, own_a, own_b, other_a, other_b, *base_a, *base_b, panel)
    return solved, pending[None, None]


def solution(mesh):
    inner = Mesh(mesh.devices.reshape(NZ, NY, NX, NCORE), ("z", "y", "x", "core"))
    row, col = ("z", "y"), ("x", "core")
    in_specs = (
        P(None, col, None, row, None, None),
        P(None, row, None, None),
        P(None, col, row, None),
        P(None, col, None, row, None),
        P(),
    )
    out_specs = (P(), P(None, col, row, None))
    return jax.shard_map(local, mesh=inner, in_specs=in_specs, out_specs=out_specs, check_vma=False)
```

```python
import functools

import jax
import jax.numpy as jnp
from jax import lax
from jax.experimental import pallas as pl
from jax.experimental.pallas import tpu as pltpu
from jax.sharding import Mesh
from jax.sharding import PartitionSpec as P

NZ, NY, NX, NCORE = 8, 4, 4, 2
SLAB = 16
HALF = 768
PART = 384
BITREV = (0, 4, 2, 6, 1, 5, 3, 7)
SHIFTS = (0, 1)
CUT = 512
BOUNDS = ((0, CUT), (CUT, HALF))


def split(x):
    high = x.astype(jnp.bfloat16)
    return high, (x - high.astype(jnp.float32)).astype(jnp.bfloat16)


def dot3(a, b):
    ah, al = split(a)
    bh, bl = split(b)
    mul = functools.partial(jnp.dot, preferred_element_type=jnp.float32)
    return mul(ah, bh) + (mul(ah, bl) + mul(al, bh))


def term_kernel(shift, z_ref, y_ref, c_ref, ea_ref, eb_ref, *refs):
    outs, acc = refs[:NY], refs[NY]
    k = pl.program_id(0)
    product = dot3(c_ref[0], jnp.concatenate([ea_ref[0], eb_ref[0]], axis=1))

    @pl.when(k == 0)
    def _():
        acc[...] = product

    @pl.when(k > 0)
    def _():
        acc[...] += product

    @pl.when(k == pl.num_programs(0) - 1)
    def _():
        label = (z_ref[0] + shift) % NZ
        for n, kz in enumerate(BITREV):
            z = ((label ^ kz) + NZ - shift) % NZ
            for ky, o_ref in enumerate(outs):
                row = pl.multiple_of((z * NY + (y_ref[0] ^ ky)) * SLAB, SLAB)
                o_ref[n] = acc[pl.ds(row, SLAB), :]


def term(z, y, coupling, earlier, chunk):
    out = pl.BlockSpec((NZ, SLAB, HALF), lambda k, z, y: (0, 0, 0))
    return pl.pallas_call(
        functools.partial(term_kernel, SHIFTS[chunk]),
        grid_spec=pltpu.PrefetchScalarGridSpec(
            num_scalar_prefetch=2,
            grid=(4,),
            in_specs=[
                pl.BlockSpec((1, 512, 512), lambda k, z, y: (k, 0, 0)),
                pl.BlockSpec((1, 512, PART), lambda k, z, y: (k, 0, chunk)),
                pl.BlockSpec((1, 512, PART), lambda k, z, y: (k, 0, 2 + chunk)),
            ],
            out_specs=(out,) * NY,
            scratch_shapes=[pltpu.VMEM((512, HALF), jnp.float32)],
        ),
        out_shape=(jax.ShapeDtypeStruct((NZ, SLAB, HALF), jnp.float32),) * NY,
        compiler_params=pltpu.CompilerParams(vmem_limit_bytes=56 * 2**20),
        cost_estimate=pl.CostEstimate(
            flops=6 * 512 * 2048 * HALF, bytes_accessed=12 * 2**20, transcendentals=0
        ),
        name="term",
    )(z, y, coupling, earlier, earlier)


def copy_in(source, target, sem):
    copy = pltpu.make_async_copy(source, target, sem)
    copy.start()
    return copy


def solve_kernel(n, y_ref, core_ref, inv_hbm, other_hbm, *refs):
    pieces, links, (o_ref, b, inv, link, sems) = refs[: -NY - 5], refs[-NY - 5 : -5], refs[-5:]
    y, core = y_ref[0], core_ref[0]
    begun = [0]

    def begin(source, target):
        begun[0] += 1
        return copy_in(source, target, sems.at[begun[0] - 1])

    def block(k):
        at = pl.ds(k * n, n)
        copies = [begin(inv_hbm.at[k], inv.at[k])]
        for ky in range(NY):
            source = pieces[ky].at[:, :, at] if len(pieces) > 1 else pieces[0].at[:, ky, :, at]
            copies.append(begin(source, b.at[k, :, y ^ ky]))
        return copies

    here = pl.ds(pl.multiple_of(core * 256, 128), 256)
    there = pl.ds(pl.multiple_of((1 - core) * 256, 128), 256)
    copies0, copies1 = block(0), block(1)
    for ky, p in enumerate(links):
        copies1.append(begin(p.at[:, :, pl.ds(p.shape[2] - 256, 256)], link.at[:, y ^ ky, :, here]))
        copies1.append(begin(other_hbm.at[ky], link.at[:, y ^ ky, :, there]))
    for copy in copies0:
        copy.wait()
    first = dot3(inv[0], b[0].reshape(512, n))
    o_ref[0] = first
    for copy in copies1:
        copy.wait()
    middle = b[1].reshape(512, n) - dot3(link[...].reshape(512, 512), first)
    o_ref[1] = dot3(inv[1], middle)


def solve(n, y, core, inverses, other, pieces, links):
    scalar, anywhere = pl.BlockSpec(memory_space=pltpu.SMEM), pl.BlockSpec(memory_space=pl.ANY)
    return pl.pallas_call(
        functools.partial(solve_kernel, n),
        in_specs=[scalar] * 2 + [anywhere] * (2 + len(pieces) + NY),
        out_specs=pl.BlockSpec(memory_space=pltpu.VMEM),
        scratch_shapes=[
            pltpu.VMEM((2, NZ, NY, SLAB, n), jnp.float32),
            pltpu.VMEM((2, 512, 512), jnp.float32),
            pltpu.VMEM((NZ, NY, SLAB, 512), jnp.float32),
            pltpu.SemaphoreType.DMA((2 + 4 * NY,)),
        ],
        out_shape=jax.ShapeDtypeStruct((2, 512, n), jnp.float32),
        compiler_params=pltpu.CompilerParams(vmem_limit_bytes=56 * 2**20),
        cost_estimate=pl.CostEstimate(
            flops=18 * 512 * 512 * n, bytes_accessed=6 * 2**20, transcendentals=0
        ),
        name="solve",
    )(y, core, inverses, other, *pieces, *links)


def columns(part, half):
    return slice(half * HALF + BOUNDS[part][0], half * HALF + BOUNDS[part][1])


def finish_kernel(chunk, core_ref, own, other, base, panel, *refs):
    solved, pending, sems = refs[-3:]
    core = core_ref[0]
    first, last = BOUNDS[chunk]
    places = ((own, core * HALF + first), (other, (1 - core) * HALF + first))
    places = [(ref, pl.ds(pl.multiple_of(at, 128), last - first)) for ref, at in places]
    copies = [copy_in(ref, solved.at[:, :, at], sems.at[i]) for i, (ref, at) in enumerate(places)]
    for half in (0, 1):
        pending[:, columns(chunk, half)] = base[:, columns(chunk, half)]
    for ref, at in places:
        update = dot3(panel[0], ref[0]) + dot3(panel[1], ref[1])
        pending[:, at] = pending[:, at] - update
    if len(refs) > 3:
        for half in (0, 1):
            pending[:, columns(1 - chunk, half)] = refs[1][:, columns(1 - chunk, half)]
    for copy in copies:
        copy.wait()


def finish(chunk, core, own, other, base, panel, *before):
    whole, anywhere = pl.BlockSpec(memory_space=pltpu.VMEM), pl.BlockSpec(memory_space=pl.ANY)
    return pl.pallas_call(
        functools.partial(finish_kernel, chunk),
        in_specs=[pl.BlockSpec(memory_space=pltpu.SMEM)] + [whole] * 4 + [anywhere, whole][: len(before)],
        out_specs=(anywhere, whole),
        scratch_shapes=[pltpu.SemaphoreType.DMA((2,))],
        out_shape=(
            jax.ShapeDtypeStruct((2, 512, 2 * HALF), jnp.float32),
            jax.ShapeDtypeStruct((SLAB, 2 * HALF), jnp.float32),
        ),
        input_output_aliases={5: 0} if before else {},
        compiler_params=pltpu.CompilerParams(vmem_limit_bytes=24 * 2**20),
        cost_estimate=pl.CostEstimate(
            flops=24 * SLAB * 512 * (BOUNDS[chunk][1] - BOUNDS[chunk][0]), bytes_accessed=6 * 2**20, transcendentals=0
        ),
        name="finish",
    )(core, own, other, base, panel, *before)


def swap(x, axis, bit, shift=0):
    n = lax.axis_size(axis)
    return lax.ppermute(x, axis, [(i, (((i + shift) % n ^ bit) - shift) % n) for i in range(n)])


def after(x, *others):
    return lax.optimization_barrier((x, *others))[0]


def sum_y(slabs):
    near = slabs[0]
    for ky in range(1, NY):
        near = near + swap(slabs[ky], "y", ky)
    return near


def sum_z(s, shift):
    for bit in (1, 2, 4):
        n = s.shape[0] // 2
        s = s[:n] + swap(s[n:], "z", bit, shift)
    return s[0]


def spread_x(v):
    others = [lax.ppermute(v, "x", [(NX - 1, i)]) for i in range(NX - 1)]
    return jnp.where(lax.axis_index("x") == NX - 1, v, others[0] + others[1] + others[2])


def gather_z(v):
    return lax.all_to_all(jnp.broadcast_to(v, (NZ, *v.shape)), "z", 0, 0, tiled=True)


def gather_y(v):
    return [v] + [swap(v, "y", ky) for ky in range(1, NY)]


def local(coupling, earlier, right_sides, panel_blocks, block_inverses):
    z, y, core = (lax.axis_index(a) for a in ("z", "y", "core"))
    coupling, earlier = coupling[0, 0, :, 0], earlier[:, 0]
    right, panel = right_sides[0, 0], panel_blocks[0, 0]
    is_first = core == 0
    z_id, y_id, core_id = (i.astype(jnp.int32).reshape(1) for i in (z, y, core))

    slabs_a = term(z_id, y_id, coupling, earlier, 0)
    slabs_b = term(z_id, y_id, after(coupling, *slabs_a), earlier, 1)
    total_a = sum_z(sum_y(slabs_a), SHIFTS[0])
    total_b = sum_z(sum_y(slabs_b), SHIFTS[1])
    base = [
        right[:, half * HALF : (half + 1) * HALF]
        - jnp.concatenate([t[:, half * PART : (half + 1) * PART] for t in (total_a, total_b)], axis=1)
        for half in (0, 1)
    ]

    kept = jnp.where(is_first, base[0], base[1])
    given = jnp.concatenate([jnp.where(is_first, base[1], base[0]), panel[0, :, 256:]], axis=1)
    came = swap(given, "core", 1)
    last = jnp.where(is_first, came[:, :HALF], kept)
    other = jnp.where(is_first, kept, came[:, :HALF])
    link = jnp.where(is_first, panel[0, :, :256], came[:, HALF:])
    v = [last[:, :CUT], other[:, :CUT], link, last[:, CUT:], other[:, CUT:]]
    v = spread_x(jnp.concatenate(v, axis=1))
    split_at = 2 * CUT + 256
    v_b = jnp.stack(gather_y(v[:, split_at:]))
    pieces_a = gather_y(after(gather_z(v[:, :split_at]), v_b))
    pieces_b = gather_z(v_b)

    part = jnp.stack([p[:, :, 2 * CUT :] for p in pieces_a])
    link = swap(part, "core", 1)
    own_a = solve(CUT, y_id, core_id, block_inverses, link, pieces_a, pieces_a)
    other_a = swap(own_a, "core", 1)
    own_b = solve(HALF - CUT, y_id, core_id, block_inverses, link, [pieces_b], pieces_a)
    other_b = swap(own_b, "core", 1)
    base = jnp.concatenate(base, axis=1)
    done_a = finish(0, core_id, own_a, other_a, base, panel)
    solved, pending = finish(1, core_id, own_b, other_b, base, panel, *done_a)
    return solved, pending[None, None]


def solution(mesh):
    inner = Mesh(mesh.devices.reshape(NZ, NY, NX, NCORE), ("z", "y", "x", "core"))
    row, col = ("z", "y"), ("x", "core")
    in_specs = (
        P(None, col, None, row, None, None),
        P(None, row, None, None),
        P(None, col, row, None),
        P(None, col, None, row, None),
        P(),
    )
    out_specs = (P(), P(None, col, row, None))
    return jax.shard_map(local, mesh=inner, in_specs=in_specs, out_specs=out_specs, check_vma=False)
```

```python
import functools

import jax
import jax.numpy as jnp
from jax import lax
from jax.experimental import pallas as pl
from jax.experimental.pallas import tpu as pltpu
from jax.sharding import Mesh
from jax.sharding import PartitionSpec as P

NZ, NY, NX, NCORE = 8, 4, 4, 2
SLAB = 16
HALF = 768
PART = 384
BITREV = (0, 4, 2, 6, 1, 5, 3, 7)
SHIFTS = (0, 1)
CUT = 512
BOUNDS = ((0, CUT), (CUT, HALF))
PLACES = ((0, 0, 8), (3, 0, 8), (1, 0, 8), (2, 0, 4), (2, 4, 4))


def split(x):
    high = x.astype(jnp.bfloat16)
    return high, (x - high.astype(jnp.float32)).astype(jnp.bfloat16)


def dot3(a, b):
    ah, al = split(a)
    bh, bl = split(b)
    mul = functools.partial(jnp.dot, preferred_element_type=jnp.float32)
    return mul(ah, bh) + (mul(ah, bl) + mul(al, bh))


def term_kernel(shift, z_ref, y_ref, c_ref, ea_ref, eb_ref, *refs):
    outs, acc = refs[:NY], refs[NY]
    k = pl.program_id(0)
    product = dot3(c_ref[0], jnp.concatenate([ea_ref[0], eb_ref[0]], axis=1))

    @pl.when(k == 0)
    def _():
        acc[...] = product

    @pl.when(k > 0)
    def _():
        acc[...] += product

    @pl.when(k == pl.num_programs(0) - 1)
    def _():
        label = (z_ref[0] + shift) % NZ
        for n, kz in enumerate(BITREV):
            z = ((label ^ kz) + NZ - shift) % NZ
            for ky, o_ref in enumerate(outs):
                row = pl.multiple_of((z * NY + (y_ref[0] ^ ky)) * SLAB, SLAB)
                o_ref[n] = acc[pl.ds(row, SLAB), :]


def term(z, y, coupling, earlier, chunk):
    out = pl.BlockSpec((NZ, SLAB, HALF), lambda k, z, y: (0, 0, 0))
    return pl.pallas_call(
        functools.partial(term_kernel, SHIFTS[chunk]),
        grid_spec=pltpu.PrefetchScalarGridSpec(
            num_scalar_prefetch=2,
            grid=(4,),
            in_specs=[
                pl.BlockSpec((1, 512, 512), lambda k, z, y: (k, 0, 0)),
                pl.BlockSpec((1, 512, PART), lambda k, z, y: (k, 0, chunk)),
                pl.BlockSpec((1, 512, PART), lambda k, z, y: (k, 0, 2 + chunk)),
            ],
            out_specs=(out,) * NY,
            scratch_shapes=[pltpu.VMEM((512, HALF), jnp.float32)],
        ),
        out_shape=(jax.ShapeDtypeStruct((NZ, SLAB, HALF), jnp.float32),) * NY,
        compiler_params=pltpu.CompilerParams(vmem_limit_bytes=56 * 2**20),
        cost_estimate=pl.CostEstimate(
            flops=6 * 512 * 2048 * HALF, bytes_accessed=12 * 2**20, transcendentals=0
        ),
        name="term",
    )(z, y, coupling, earlier, earlier)


def copy_in(source, target, sem):
    copy = pltpu.make_async_copy(source, target, sem)
    copy.start()
    return copy


def solve_kernel(n, y_ref, core_ref, inv_hbm, other_hbm, *refs):
    pieces, links, (o_ref, b, inv, link, sems) = refs[:-10], refs[-10:-5], refs[-5:]
    y, core = y_ref[0], core_ref[0]
    begun = [0]

    def begin(source, target):
        begun[0] += 1
        return copy_in(source, target, sems.at[begun[0] - 1])

    def block(k):
        at = pl.ds(k * n, n)
        copies = [begin(inv_hbm.at[k], inv.at[k])]
        if len(pieces) > 1:
            for p, (by, z, count) in zip(pieces, PLACES):
                copies.append(begin(p.at[:, :, at], b.at[k, pl.ds(z, count), (y + by) % NY]))
        else:
            for ky in range(NY):
                copies.append(begin(pieces[0].at[:, ky, :, at], b.at[k, :, y ^ ky]))
        return copies

    here = pl.ds(pl.multiple_of(core * 256, 128), 256)
    there = pl.ds(pl.multiple_of((1 - core) * 256, 128), 256)
    copies0, copies1 = block(0), block(1)
    for p, (by, z, count) in zip(links, PLACES):
        target = link.at[pl.ds(z, count), (y + by) % NY]
        copies1.append(begin(p.at[:, :, pl.ds(p.shape[2] - 256, 256)], target.at[:, :, here]))
    for i, by in enumerate((0, -1, 1, 2)):
        copies1.append(begin(other_hbm.at[i], link.at[:, (y + by + NY) % NY, :, there]))
    for copy in copies0:
        copy.wait()
    first = dot3(inv[0], b[0].reshape(512, n))
    o_ref[0] = first
    for copy in copies1:
        copy.wait()
    middle = b[1].reshape(512, n) - dot3(link[...].reshape(512, 512), first)
    o_ref[1] = dot3(inv[1], middle)


def solve(n, y, core, inverses, other, pieces, links):
    scalar, anywhere = pl.BlockSpec(memory_space=pltpu.SMEM), pl.BlockSpec(memory_space=pl.ANY)
    return pl.pallas_call(
        functools.partial(solve_kernel, n),
        in_specs=[scalar] * 2 + [anywhere] * (2 + len(pieces) + len(links)),
        out_specs=pl.BlockSpec(memory_space=pltpu.VMEM),
        scratch_shapes=[
            pltpu.VMEM((2, NZ, NY, SLAB, n), jnp.float32),
            pltpu.VMEM((2, 512, 512), jnp.float32),
            pltpu.VMEM((NZ, NY, SLAB, 512), jnp.float32),
            pltpu.SemaphoreType.DMA((21,)),
        ],
        out_shape=jax.ShapeDtypeStruct((2, 512, n), jnp.float32),
        compiler_params=pltpu.CompilerParams(vmem_limit_bytes=60 * 2**20),
        cost_estimate=pl.CostEstimate(
            flops=18 * 512 * 512 * n, bytes_accessed=6 * 2**20, transcendentals=0
        ),
        name="solve",
    )(y, core, inverses, other, *pieces, *links)


def columns(part, half):
    return slice(half * HALF + BOUNDS[part][0], half * HALF + BOUNDS[part][1])


def finish_kernel(chunk, core_ref, own, other, base, panel, *refs):
    solved, pending, sems = refs[-3:]
    core = core_ref[0]
    first, last = BOUNDS[chunk]
    places = ((own, core * HALF + first), (other, (1 - core) * HALF + first))
    places = [(ref, pl.ds(pl.multiple_of(at, 128), last - first)) for ref, at in places]
    copies = [copy_in(ref, solved.at[:, :, at], sems.at[i]) for i, (ref, at) in enumerate(places)]
    for half in (0, 1):
        pending[:, columns(chunk, half)] = base[:, columns(chunk, half)]
    for ref, at in places:
        update = dot3(panel[0], ref[0]) + dot3(panel[1], ref[1])
        pending[:, at] = pending[:, at] - update
    if len(refs) > 3:
        for half in (0, 1):
            pending[:, columns(1 - chunk, half)] = refs[1][:, columns(1 - chunk, half)]
    for copy in copies:
        copy.wait()


def finish(chunk, core, own, other, base, panel, *before):
    whole, anywhere = pl.BlockSpec(memory_space=pltpu.VMEM), pl.BlockSpec(memory_space=pl.ANY)
    return pl.pallas_call(
        functools.partial(finish_kernel, chunk),
        in_specs=[pl.BlockSpec(memory_space=pltpu.SMEM)] + [whole] * 4 + [anywhere, whole][: len(before)],
        out_specs=(anywhere, whole),
        scratch_shapes=[pltpu.SemaphoreType.DMA((2,))],
        out_shape=(
            jax.ShapeDtypeStruct((2, 512, 2 * HALF), jnp.float32),
            jax.ShapeDtypeStruct((SLAB, 2 * HALF), jnp.float32),
        ),
        input_output_aliases={5: 0} if before else {},
        compiler_params=pltpu.CompilerParams(vmem_limit_bytes=24 * 2**20),
        cost_estimate=pl.CostEstimate(
            flops=24 * SLAB * 512 * (BOUNDS[chunk][1] - BOUNDS[chunk][0]), bytes_accessed=6 * 2**20, transcendentals=0
        ),
        name="finish",
    )(core, own, other, base, panel, *before)


def swap(x, axis, bit, shift=0):
    n = lax.axis_size(axis)
    return lax.ppermute(x, axis, [(i, (((i + shift) % n ^ bit) - shift) % n) for i in range(n)])


def after(x, *others):
    return lax.optimization_barrier((x, *others))[0]


def sum_y(slabs):
    near = slabs[0]
    for ky in range(1, NY):
        near = near + swap(slabs[ky], "y", ky)
    return near


def halve(s, bit, shift):
    n = s.shape[0] // 2
    return s[:n] + swap(s[n:], "z", bit, shift)


def sum_z(s, shift):
    for bit in (1, 2, 4):
        s = halve(s, bit, shift)
    return s[0]


def spread_x(v):
    others = [lax.ppermute(v, "x", [(NX - 1, i)]) for i in range(NX - 1)]
    return jnp.where(lax.axis_index("x") == NX - 1, v, others[0] + others[1] + others[2])


def gather_z(v):
    return lax.all_to_all(jnp.broadcast_to(v, (NZ, *v.shape)), "z", 0, 0, tiled=True)


def gather_y(v):
    return [v] + [swap(v, "y", ky) for ky in range(1, NY)]


def step(x, axis, by):
    n = lax.axis_size(axis)
    return lax.ppermute(x, axis, [(i, (i + by) % n) for i in range(n)])


def gather_y_twice(v):
    up, down = step(v, "y", 1), step(v, "y", -1)
    h = NZ // 2
    return [v, up, down, step(up[:h], "y", 1), step(down[h:], "y", -1)]


def local(coupling, earlier, right_sides, panel_blocks, block_inverses):
    z, y, core = (lax.axis_index(a) for a in ("z", "y", "core"))
    coupling, earlier = coupling[0, 0, :, 0], earlier[:, 0]
    right, panel = right_sides[0, 0], panel_blocks[0, 0]
    is_first = core == 0
    z_id, y_id, core_id = (i.astype(jnp.int32).reshape(1) for i in (z, y, core))

    slabs_a = term(z_id, y_id, coupling, earlier, 0)
    slabs_b = term(z_id, y_id, after(coupling, *slabs_a), earlier, 1)
    near_a = halve(sum_y(slabs_a), 1, SHIFTS[0])
    near_b = sum_y([after(slabs_b[0], near_a), *slabs_b[1:]])
    total_a = halve(halve(near_a, 2, SHIFTS[0]), 4, SHIFTS[0])[0]
    total_b = sum_z(near_b, SHIFTS[1])
    base = [
        right[:, half * HALF : (half + 1) * HALF]
        - jnp.concatenate([t[:, half * PART : (half + 1) * PART] for t in (total_a, total_b)], axis=1)
        for half in (0, 1)
    ]

    kept = jnp.where(is_first, base[0], base[1])
    given = jnp.concatenate([jnp.where(is_first, base[1], base[0]), panel[0, :, 256:]], axis=1)
    came = swap(given, "core", 1)
    last = jnp.where(is_first, came[:, :HALF], kept)
    other = jnp.where(is_first, kept, came[:, :HALF])
    link = jnp.where(is_first, panel[0, :, :256], came[:, HALF:])
    v = [last[:, :CUT], other[:, :CUT], link, last[:, CUT:], other[:, CUT:]]
    v = spread_x(jnp.concatenate(v, axis=1))
    split_at = 2 * CUT + 256
    v_b = jnp.stack(gather_y(v[:, split_at:]))
    pieces_a = gather_y_twice(after(gather_z(v[:, :split_at]), v_b))
    pieces_b = gather_z(v_b)

    part = jnp.concatenate([p[:, :, 2 * CUT :] for p in pieces_a]).reshape(NY, NZ, SLAB, 256)
    link = swap(part, "core", 1)
    own_a = solve(CUT, y_id, core_id, block_inverses, link, pieces_a, pieces_a)
    other_a = swap(own_a, "core", 1)
    own_b = solve(HALF - CUT, y_id, core_id, block_inverses, link, [pieces_b], pieces_a)
    other_b = swap(own_b, "core", 1)
    base = jnp.concatenate(base, axis=1)
    done_a = finish(0, core_id, own_a, other_a, base, panel)
    solved, pending = finish(1, core_id, own_b, other_b, base, panel, *done_a)
    return solved, pending[None, None]


def solution(mesh):
    inner = Mesh(mesh.devices.reshape(NZ, NY, NX, NCORE), ("z", "y", "x", "core"))
    row, col = ("z", "y"), ("x", "core")
    in_specs = (
        P(None, col, None, row, None, None),
        P(None, row, None, None),
        P(None, col, row, None),
        P(None, col, None, row, None),
        P(),
    )
    out_specs = (P(), P(None, col, row, None))
    return jax.shard_map(local, mesh=inner, in_specs=in_specs, out_specs=out_specs, check_vma=False)
```

```python
import functools

import jax
import jax.numpy as jnp
from jax import lax
from jax.experimental import pallas as pl
from jax.experimental.pallas import tpu as pltpu
from jax.sharding import Mesh
from jax.sharding import PartitionSpec as P

NZ, NY, NX, NCORE = 8, 4, 4, 2
SLAB = 16
HALF = 768
BITREV = (0, 4, 2, 6, 1, 5, 3, 7)
SHIFTS = (0, 1)
STRIP = 256
CUT = 512
BOUNDS = ((0, CUT), (CUT, HALF))
PLACES = ((0, 0, 8), (3, 0, 8), (1, 0, 8), (2, 0, 4), (2, 4, 4))


def split(x):
    high = x.astype(jnp.bfloat16)
    return high, (x - high.astype(jnp.float32)).astype(jnp.bfloat16)


def dot3(a, b):
    ah, al = split(a)
    bh, bl = split(b)
    mul = functools.partial(jnp.dot, preferred_element_type=jnp.float32)
    return mul(ah, bh) + (mul(ah, bl) + mul(al, bh))


def width(part):
    return BOUNDS[part][1] - BOUNDS[part][0]


def term_kernel(part, z_ref, y_ref, c_ref, *refs):
    strips, outs, acc = refs[: -NY - 1], refs[-NY - 1 : -1], refs[-1]
    k = pl.program_id(0)
    product = dot3(c_ref[0], jnp.concatenate([e[0] for e in strips], axis=1))

    @pl.when(k == 0)
    def _():
        acc[...] = product

    @pl.when(k > 0)
    def _():
        acc[...] += product

    @pl.when(k == pl.num_programs(0) - 1)
    def _():
        shift = SHIFTS[part]
        label = (z_ref[0] + shift) % NZ
        for n, kz in enumerate(BITREV):
            z = ((label ^ kz) + NZ - shift) % NZ
            for ky, o_ref in enumerate(outs):
                row = pl.multiple_of((z * NY + (y_ref[0] ^ ky)) * SLAB, SLAB)
                o_ref[n] = acc[pl.ds(row, SLAB), :]


def term(z, y, coupling, earlier, part):
    n = 2 * width(part)
    at = BOUNDS[part][0] // STRIP
    strips = [half * (HALF // STRIP) + at + i for half in (0, 1) for i in range(width(part) // STRIP)]
    out = pl.BlockSpec((NZ, SLAB, n), lambda k, z, y: (0, 0, 0))
    return pl.pallas_call(
        functools.partial(term_kernel, part),
        grid_spec=pltpu.PrefetchScalarGridSpec(
            num_scalar_prefetch=2,
            grid=(4,),
            in_specs=[pl.BlockSpec((1, 512, 512), lambda k, z, y: (k, 0, 0))]
            + [pl.BlockSpec((1, 512, STRIP), lambda k, z, y, i=i: (k, 0, i)) for i in strips],
            out_specs=(out,) * NY,
            scratch_shapes=[pltpu.VMEM((512, n), jnp.float32)],
        ),
        out_shape=(jax.ShapeDtypeStruct((NZ, SLAB, n), jnp.float32),) * NY,
        compiler_params=pltpu.CompilerParams(vmem_limit_bytes=56 * 2**20),
        cost_estimate=pl.CostEstimate(
            flops=6 * 512 * 2048 * n, bytes_accessed=2**22 + 2**13 * n, transcendentals=0
        ),
        name="term",
    )(z, y, coupling, *[earlier] * len(strips))


def copy_in(source, target, sem):
    copy = pltpu.make_async_copy(source, target, sem)
    copy.start()
    return copy


def solve_kernel(n, y_ref, core_ref, inv_hbm, other_hbm, *refs):
    pieces, links, (o_ref, b, inv, link, sems) = refs[:-10], refs[-10:-5], refs[-5:]
    y, core = y_ref[0], core_ref[0]
    begun = [0]

    def begin(source, target):
        begun[0] += 1
        return copy_in(source, target, sems.at[begun[0] - 1])

    def block(k):
        at = pl.ds(k * n, n)
        copies = [begin(inv_hbm.at[k], inv.at[k])]
        if len(pieces) > 1:
            for p, (by, z, count) in zip(pieces, PLACES):
                copies.append(begin(p.at[:, :, at], b.at[k, pl.ds(z, count), (y + by) % NY]))
        else:
            for ky in range(NY):
                copies.append(begin(pieces[0].at[:, ky, :, at], b.at[k, :, y ^ ky]))
        return copies

    here = pl.ds(pl.multiple_of(core * 256, 128), 256)
    there = pl.ds(pl.multiple_of((1 - core) * 256, 128), 256)
    copies0, copies1 = block(0), block(1)
    for p, (by, z, count) in zip(links, PLACES):
        target = link.at[pl.ds(z, count), (y + by) % NY]
        copies1.append(begin(p.at[:, :, pl.ds(p.shape[2] - 256, 256)], target.at[:, :, here]))
    for i, by in enumerate((0, -1, 1, 2)):
        copies1.append(begin(other_hbm.at[i], link.at[:, (y + by + NY) % NY, :, there]))
    for copy in copies0:
        copy.wait()
    first = dot3(inv[0], b[0].reshape(512, n))
    o_ref[0] = first
    for copy in copies1:
        copy.wait()
    middle = b[1].reshape(512, n) - dot3(link[...].reshape(512, 512), first)
    o_ref[1] = dot3(inv[1], middle)


def solve(n, y, core, inverses, other, pieces, links):
    scalar, anywhere = pl.BlockSpec(memory_space=pltpu.SMEM), pl.BlockSpec(memory_space=pl.ANY)
    return pl.pallas_call(
        functools.partial(solve_kernel, n),
        in_specs=[scalar] * 2 + [anywhere] * (2 + len(pieces) + len(links)),
        out_specs=pl.BlockSpec(memory_space=pltpu.VMEM),
        scratch_shapes=[
            pltpu.VMEM((2, NZ, NY, SLAB, n), jnp.float32),
            pltpu.VMEM((2, 512, 512), jnp.float32),
            pltpu.VMEM((NZ, NY, SLAB, 512), jnp.float32),
            pltpu.SemaphoreType.DMA((21,)),
        ],
        out_shape=jax.ShapeDtypeStruct((2, 512, n), jnp.float32),
        compiler_params=pltpu.CompilerParams(vmem_limit_bytes=60 * 2**20),
        cost_estimate=pl.CostEstimate(
            flops=18 * 512 * 512 * n, bytes_accessed=6 * 2**20, transcendentals=0
        ),
        name="solve",
    )(y, core, inverses, other, *pieces, *links)


def columns(part, half):
    return slice(half * HALF + BOUNDS[part][0], half * HALF + BOUNDS[part][1])


def finish_kernel(chunk, core_ref, own, other, base, panel, *refs):
    solved, pending, sems = refs[-3:]
    core = core_ref[0]
    first, last = BOUNDS[chunk]
    places = ((own, core * HALF + first), (other, (1 - core) * HALF + first))
    places = [(ref, pl.ds(pl.multiple_of(at, 128), last - first)) for ref, at in places]
    copies = [copy_in(ref, solved.at[:, :, at], sems.at[i]) for i, (ref, at) in enumerate(places)]
    for half in (0, 1):
        pending[:, columns(chunk, half)] = base[:, half * (last - first) : (half + 1) * (last - first)]
    for ref, at in places:
        update = dot3(panel[0], ref[0]) + dot3(panel[1], ref[1])
        pending[:, at] = pending[:, at] - update
    if len(refs) > 3:
        for half in (0, 1):
            pending[:, columns(1 - chunk, half)] = refs[1][:, columns(1 - chunk, half)]
    for copy in copies:
        copy.wait()


def finish(chunk, core, own, other, base, panel, *before):
    whole, anywhere = pl.BlockSpec(memory_space=pltpu.VMEM), pl.BlockSpec(memory_space=pl.ANY)
    return pl.pallas_call(
        functools.partial(finish_kernel, chunk),
        in_specs=[pl.BlockSpec(memory_space=pltpu.SMEM)] + [whole] * 4 + [anywhere, whole][: len(before)],
        out_specs=(anywhere, whole),
        scratch_shapes=[pltpu.SemaphoreType.DMA((2,))],
        out_shape=(
            jax.ShapeDtypeStruct((2, 512, 2 * HALF), jnp.float32),
            jax.ShapeDtypeStruct((SLAB, 2 * HALF), jnp.float32),
        ),
        input_output_aliases={5: 0} if before else {},
        compiler_params=pltpu.CompilerParams(vmem_limit_bytes=24 * 2**20),
        cost_estimate=pl.CostEstimate(
            flops=24 * SLAB * 512 * (BOUNDS[chunk][1] - BOUNDS[chunk][0]), bytes_accessed=6 * 2**20, transcendentals=0
        ),
        name="finish",
    )(core, own, other, base, panel, *before)


def swap(x, axis, bit, shift=0):
    n = lax.axis_size(axis)
    return lax.ppermute(x, axis, [(i, (((i + shift) % n ^ bit) - shift) % n) for i in range(n)])


def after(x, *others):
    return lax.optimization_barrier((x, *others))[0]


def sum_y(slabs):
    near = slabs[0]
    for ky in range(1, NY):
        near = near + swap(slabs[ky], "y", ky)
    return near


def halve(s, bit, shift):
    n = s.shape[0] // 2
    return s[:n] + swap(s[n:], "z", bit, shift)


def sum_z(s, shift):
    for bit in (1, 2, 4):
        s = halve(s, bit, shift)
    return s[0]


def spread_x(v):
    others = [lax.ppermute(v, "x", [(NX - 1, i)]) for i in range(NX - 1)]
    return jnp.where(lax.axis_index("x") == NX - 1, v, others[0] + others[1] + others[2])


def gather_z(v):
    return lax.all_to_all(jnp.broadcast_to(v, (NZ, *v.shape)), "z", 0, 0, tiled=True)


def gather_y(v):
    return [v] + [swap(v, "y", ky) for ky in range(1, NY)]


def step(x, axis, by):
    n = lax.axis_size(axis)
    return lax.ppermute(x, axis, [(i, (i + by) % n) for i in range(n)])


def gather_y_twice(v):
    up, down = step(v, "y", 1), step(v, "y", -1)
    h = NZ // 2
    return [v, up, down, step(up[:h], "y", 1), step(down[h:], "y", -1)]


def local(coupling, earlier, right_sides, panel_blocks, block_inverses):
    z, y, core = (lax.axis_index(a) for a in ("z", "y", "core"))
    coupling, earlier = coupling[0, 0, :, 0], earlier[:, 0]
    right, panel = right_sides[0, 0], panel_blocks[0, 0]
    is_first = core == 0
    z_id, y_id, core_id = (i.astype(jnp.int32).reshape(1) for i in (z, y, core))

    slabs_a = term(z_id, y_id, coupling, earlier, 0)
    slabs_b = term(z_id, y_id, after(coupling, *slabs_a), earlier, 1)
    near_a = halve(sum_y(slabs_a), 1, SHIFTS[0])
    near_b = sum_y([after(slabs_b[0], near_a), *slabs_b[1:]])
    total_a = halve(halve(near_a, 2, SHIFTS[0]), 4, SHIFTS[0])[0]
    total_b = sum_z(near_b, SHIFTS[1])
    def subtract(total, part):
        return jnp.concatenate([right[:, columns(part, half)] for half in (0, 1)], axis=1) - total

    def exchange(base, extra):
        n = base.shape[1] // 2
        kept = jnp.where(is_first, base[:, :n], base[:, n:])
        given = jnp.where(is_first, base[:, n:], base[:, :n])
        if extra is not None:
            given = jnp.concatenate([given, extra[:, 256:]], axis=1)
        came = swap(given, "core", 1)
        v = [jnp.where(is_first, came[:, :n], kept), jnp.where(is_first, kept, came[:, :n])]
        if extra is not None:
            v.append(jnp.where(is_first, extra[:, :256], came[:, n:]))
        return jnp.concatenate(v, axis=1)

    base_a, base_b = subtract(total_a, 0), subtract(total_b, 1)
    v_a = gather_z(spread_x(exchange(base_a, panel[0])))
    v_b = jnp.stack(gather_y(spread_x(exchange(base_b, None))))
    pieces_a = gather_y_twice(after(v_a, v_b))
    pieces_b = gather_z(v_b)

    part = jnp.concatenate([p[:, :, 2 * CUT :] for p in pieces_a]).reshape(NY, NZ, SLAB, 256)
    link = swap(part, "core", 1)
    own_a = solve(CUT, y_id, core_id, block_inverses, link, pieces_a, pieces_a)
    other_a = swap(own_a, "core", 1)
    own_b = solve(HALF - CUT, y_id, core_id, block_inverses, link, [pieces_b], pieces_a)
    other_b = swap(own_b, "core", 1)
    done_a = finish(0, core_id, own_a, other_a, base_a, panel)
    solved, pending = finish(1, core_id, own_b, other_b, base_b, panel, *done_a)
    return solved, pending[None, None]


def solution(mesh):
    inner = Mesh(mesh.devices.reshape(NZ, NY, NX, NCORE), ("z", "y", "x", "core"))
    row, col = ("z", "y"), ("x", "core")
    in_specs = (
        P(None, col, None, row, None, None),
        P(None, row, None, None),
        P(None, col, row, None),
        P(None, col, None, row, None),
        P(),
    )
    out_specs = (P(), P(None, col, row, None))
    return jax.shard_map(local, mesh=inner, in_specs=in_specs, out_specs=out_specs, check_vma=False)
```

```python
import functools

import jax
import jax.numpy as jnp
from jax import lax
from jax.experimental import pallas as pl
from jax.experimental.pallas import tpu as pltpu
from jax.sharding import Mesh
from jax.sharding import PartitionSpec as P

NZ, NY, NX, NCORE = 8, 4, 4, 2
SLAB = 16
HALF = 768
BITREV = (0, 4, 2, 6, 1, 5, 3, 7)
SHIFTS = (0, 1)
STRIP = 256
CUT = 512
BOUNDS = ((0, CUT), (CUT, HALF))
PLACES = ((0, 0, 8), (3, 0, 8), (1, 0, 8), (2, 0, 4), (2, 4, 4))


def split(x):
    high = x.astype(jnp.bfloat16)
    return high, (x - high.astype(jnp.float32)).astype(jnp.bfloat16)


def dot3(a, b):
    ah, al = split(a)
    bh, bl = split(b)
    mul = functools.partial(jnp.dot, preferred_element_type=jnp.float32)
    return mul(ah, bh) + (mul(ah, bl) + mul(al, bh))


def width(part):
    return BOUNDS[part][1] - BOUNDS[part][0]


def term_kernel(part, z_ref, y_ref, c_ref, *refs):
    strips, outs, acc = refs[: -NY - 1], refs[-NY - 1 : -1], refs[-1]
    k = pl.program_id(0)
    product = dot3(c_ref[0], jnp.concatenate([e[0] for e in strips], axis=1))

    @pl.when(k == 0)
    def _():
        acc[...] = product

    @pl.when(k > 0)
    def _():
        acc[...] += product

    @pl.when(k == pl.num_programs(0) - 1)
    def _():
        shift = SHIFTS[part]
        label = (z_ref[0] + shift) % NZ
        for n, kz in enumerate(BITREV):
            z = ((label ^ kz) + NZ - shift) % NZ
            for ky, o_ref in enumerate(outs):
                row = pl.multiple_of((z * NY + (y_ref[0] ^ ky)) * SLAB, SLAB)
                o_ref[n] = acc[pl.ds(row, SLAB), :]


def term(z, y, coupling, earlier, part):
    n = 2 * width(part)
    at = BOUNDS[part][0] // STRIP
    strips = [half * (HALF // STRIP) + at + i for half in (0, 1) for i in range(width(part) // STRIP)]
    out = pl.BlockSpec((NZ, SLAB, n), lambda k, z, y: (0, 0, 0))
    return pl.pallas_call(
        functools.partial(term_kernel, part),
        grid_spec=pltpu.PrefetchScalarGridSpec(
            num_scalar_prefetch=2,
            grid=(4,),
            in_specs=[pl.BlockSpec((1, 512, 512), lambda k, z, y: (k, 0, 0))]
            + [pl.BlockSpec((1, 512, STRIP), lambda k, z, y, i=i: (k, 0, i)) for i in strips],
            out_specs=(out,) * NY,
            scratch_shapes=[pltpu.VMEM((512, n), jnp.float32)],
        ),
        out_shape=(jax.ShapeDtypeStruct((NZ, SLAB, n), jnp.float32),) * NY,
        compiler_params=pltpu.CompilerParams(vmem_limit_bytes=56 * 2**20),
        cost_estimate=pl.CostEstimate(
            flops=6 * 512 * 2048 * n, bytes_accessed=2**22 + 2**13 * n, transcendentals=0
        ),
        name="term",
    )(z, y, coupling, *[earlier] * len(strips))


def copy_in(source, target, sem):
    copy = pltpu.make_async_copy(source, target, sem)
    copy.start()
    return copy


def solve_kernel(n, y_ref, core_ref, inv_hbm, other_hbm, *refs):
    pieces, links, (o_ref, b, inv, link, sems) = refs[:-10], refs[-10:-5], refs[-5:]
    y, core = y_ref[0], core_ref[0]
    begun = [0]

    def begin(source, target):
        begun[0] += 1
        return copy_in(source, target, sems.at[begun[0] - 1])

    def block(k):
        at = pl.ds(k * n, n)
        copies = [begin(inv_hbm.at[k], inv.at[k])]
        if len(pieces) > 1:
            for p, (by, z, count) in zip(pieces, PLACES):
                copies.append(begin(p.at[:, :, at], b.at[k, pl.ds(z, count), (y + by) % NY]))
        else:
            for ky in range(NY):
                copies.append(begin(pieces[0].at[:, ky, :, at], b.at[k, :, y ^ ky]))
        return copies

    here = pl.ds(pl.multiple_of(core * 256, 128), 256)
    there = pl.ds(pl.multiple_of((1 - core) * 256, 128), 256)
    copies0, copies1 = block(0), block(1)
    for p, (by, z, count) in zip(links, PLACES):
        target = link.at[pl.ds(z, count), (y + by) % NY]
        copies1.append(begin(p.at[:, :, pl.ds(p.shape[2] - 256, 256)], target.at[:, :, here]))
    for i, by in enumerate((0, -1, 1, 2)):
        copies1.append(begin(other_hbm.at[i], link.at[:, (y + by + NY) % NY, :, there]))
    for copy in copies0:
        copy.wait()
    first = dot3(inv[0], b[0].reshape(512, n))
    o_ref[0] = first
    for copy in copies1:
        copy.wait()
    middle = b[1].reshape(512, n) - dot3(link[...].reshape(512, 512), first)
    o_ref[1] = dot3(inv[1], middle)


def solve(n, y, core, inverses, other, pieces, links):
    scalar, anywhere = pl.BlockSpec(memory_space=pltpu.SMEM), pl.BlockSpec(memory_space=pl.ANY)
    return pl.pallas_call(
        functools.partial(solve_kernel, n),
        in_specs=[scalar] * 2 + [anywhere] * (2 + len(pieces) + len(links)),
        out_specs=pl.BlockSpec(memory_space=pltpu.VMEM),
        scratch_shapes=[
            pltpu.VMEM((2, NZ, NY, SLAB, n), jnp.float32),
            pltpu.VMEM((2, 512, 512), jnp.float32),
            pltpu.VMEM((NZ, NY, SLAB, 512), jnp.float32),
            pltpu.SemaphoreType.DMA((21,)),
        ],
        out_shape=jax.ShapeDtypeStruct((2, 512, n), jnp.float32),
        compiler_params=pltpu.CompilerParams(vmem_limit_bytes=60 * 2**20),
        cost_estimate=pl.CostEstimate(
            flops=18 * 512 * 512 * n, bytes_accessed=6 * 2**20, transcendentals=0
        ),
        name="solve",
    )(y, core, inverses, other, *pieces, *links)


def columns(part, half):
    return slice(half * HALF + BOUNDS[part][0], half * HALF + BOUNDS[part][1])


def finish_kernel(chunk, core_ref, own, other, base, panel, *refs):
    solved, pending, sems = refs[-3:]
    core = core_ref[0]
    first, last = BOUNDS[chunk]
    places = ((own, core * HALF + first), (other, (1 - core) * HALF + first))
    places = [(ref, pl.ds(pl.multiple_of(at, 128), last - first)) for ref, at in places]
    copies = [copy_in(ref, solved.at[:, :, at], sems.at[i]) for i, (ref, at) in enumerate(places)]
    for half in (0, 1):
        pending[:, columns(chunk, half)] = base[:, half * (last - first) : (half + 1) * (last - first)]
    for ref, at in places:
        update = dot3(panel[0], ref[0]) + dot3(panel[1], ref[1])
        pending[:, at] = pending[:, at] - update
    if len(refs) > 3:
        for half in (0, 1):
            pending[:, columns(1 - chunk, half)] = refs[1][:, columns(1 - chunk, half)]
    for copy in copies:
        copy.wait()


def finish(chunk, core, own, other, base, panel, *before):
    whole, anywhere = pl.BlockSpec(memory_space=pltpu.VMEM), pl.BlockSpec(memory_space=pl.ANY)
    return pl.pallas_call(
        functools.partial(finish_kernel, chunk),
        in_specs=[pl.BlockSpec(memory_space=pltpu.SMEM)] + [whole] * 4 + [anywhere, whole][: len(before)],
        out_specs=(anywhere, whole),
        scratch_shapes=[pltpu.SemaphoreType.DMA((2,))],
        out_shape=(
            jax.ShapeDtypeStruct((2, 512, 2 * HALF), jnp.float32),
            jax.ShapeDtypeStruct((SLAB, 2 * HALF), jnp.float32),
        ),
        input_output_aliases={5: 0} if before else {},
        compiler_params=pltpu.CompilerParams(vmem_limit_bytes=24 * 2**20),
        cost_estimate=pl.CostEstimate(
            flops=24 * SLAB * 512 * (BOUNDS[chunk][1] - BOUNDS[chunk][0]), bytes_accessed=6 * 2**20, transcendentals=0
        ),
        name="finish",
    )(core, own, other, base, panel, *before)


def swap(x, axis, bit, shift=0):
    n = lax.axis_size(axis)
    return lax.ppermute(x, axis, [(i, (((i + shift) % n ^ bit) - shift) % n) for i in range(n)])


def after(x, *others):
    return lax.optimization_barrier((x, *others))[0]


def sum_y(slabs):
    near = slabs[0]
    for ky in range(1, NY):
        near = near + swap(slabs[ky], "y", ky)
    return near


def halve(s, bit, shift):
    n = s.shape[0] // 2
    return s[:n] + swap(s[n:], "z", bit, shift)


def sum_z(s, shift):
    for bit in (1, 2, 4):
        s = halve(s, bit, shift)
    return s[0]


def spread_x(v):
    others = [lax.ppermute(v, "x", [(NX - 1, i)]) for i in (2, 0, 1)]
    return jnp.where(lax.axis_index("x") == NX - 1, v, others[0] + others[1] + others[2])


def gather_z(v):
    return lax.all_to_all(jnp.broadcast_to(v, (NZ, *v.shape)), "z", 0, 0, tiled=True)


def gather_y(v):
    return [v] + [swap(v, "y", ky) for ky in range(1, NY)]


def step(x, axis, by):
    n = lax.axis_size(axis)
    return lax.ppermute(x, axis, [(i, (i + by) % n) for i in range(n)])


def gather_y_twice(v):
    up, down = step(v, "y", 1), step(v, "y", -1)
    h = NZ // 2
    return [v, up, down, step(up[:h], "y", 1), step(down[h:], "y", -1)]


def local(coupling, earlier, right_sides, panel_blocks, block_inverses):
    z, y, core = (lax.axis_index(a) for a in ("z", "y", "core"))
    coupling, earlier = coupling[0, 0, :, 0], earlier[:, 0]
    right, panel = right_sides[0, 0], panel_blocks[0, 0]
    is_first = core == 0
    z_id, y_id, core_id = (i.astype(jnp.int32).reshape(1) for i in (z, y, core))

    slabs_a = term(z_id, y_id, coupling, earlier, 0)
    slabs_b = term(z_id, y_id, after(coupling, *slabs_a), earlier, 1)
    near_a = halve(sum_y(slabs_a), 1, SHIFTS[0])
    near_b = sum_y([after(slabs_b[0], near_a), *slabs_b[1:]])
    total_a = halve(halve(near_a, 2, SHIFTS[0]), 4, SHIFTS[0])[0]
    total_b = sum_z(near_b, SHIFTS[1])
    def subtract(total, part):
        return jnp.concatenate([right[:, columns(part, half)] for half in (0, 1)], axis=1) - total

    def exchange(base, extra):
        n = base.shape[1] // 2
        kept = jnp.where(is_first, base[:, :n], base[:, n:])
        given = jnp.where(is_first, base[:, n:], base[:, :n])
        if extra is not None:
            given = jnp.concatenate([given, extra[:, 256:]], axis=1)
        came = swap(given, "core", 1)
        v = [jnp.where(is_first, came[:, :n], kept), jnp.where(is_first, kept, came[:, :n])]
        if extra is not None:
            v.append(jnp.where(is_first, extra[:, :256], came[:, n:]))
        return jnp.concatenate(v, axis=1)

    base_a, base_b = subtract(total_a, 0), subtract(total_b, 1)
    v_a = gather_z(spread_x(exchange(base_a, panel[0])))
    v_b = jnp.stack(gather_y(spread_x(exchange(base_b, None))))
    pieces_a = gather_y_twice(after(v_a, v_b))
    pieces_b = gather_z(v_b)

    part = jnp.concatenate([p[:, :, 2 * CUT :] for p in pieces_a]).reshape(NY, NZ, SLAB, 256)
    link = swap(part, "core", 1)
    own_a = solve(CUT, y_id, core_id, block_inverses, link, pieces_a, pieces_a)
    other_a = swap(own_a, "core", 1)
    own_b = solve(HALF - CUT, y_id, core_id, block_inverses, link, [pieces_b], pieces_a)
    other_b = swap(own_b, "core", 1)
    done_a = finish(0, core_id, own_a, other_a, base_a, panel)
    solved, pending = finish(1, core_id, own_b, other_b, base_b, panel, *done_a)
    return solved, pending[None, None]


def solution(mesh):
    inner = Mesh(mesh.devices.reshape(NZ, NY, NX, NCORE), ("z", "y", "x", "core"))
    row, col = ("z", "y"), ("x", "core")
    in_specs = (
        P(None, col, None, row, None, None),
        P(None, row, None, None),
        P(None, col, row, None),
        P(None, col, None, row, None),
        P(),
    )
    out_specs = (P(), P(None, col, row, None))
    return jax.shard_map(local, mesh=inner, in_specs=in_specs, out_specs=out_specs, check_vma=False)
```

```python
import functools

import jax
import jax.numpy as jnp
from jax import lax
from jax.experimental import pallas as pl
from jax.experimental.pallas import tpu as pltpu
from jax.sharding import Mesh
from jax.sharding import PartitionSpec as P

NZ, NY, NX, NCORE = 8, 4, 4, 2
SLAB = 16
HALF = 768
BITREV = (0, 4, 2, 6, 1, 5, 3, 7)
SHIFTS = (0, 1)
STRIP = 256
CUT = 512
BOUNDS = ((0, CUT), (CUT, HALF))
PLACES = ((0, 0, 8), (3, 0, 8), (1, 0, 8), (2, 0, 4), (2, 4, 4))


def split(x):
    high = x.astype(jnp.bfloat16)
    return high, (x - high.astype(jnp.float32)).astype(jnp.bfloat16)


def dot3(a, b):
    ah, al = split(a)
    bh, bl = split(b)
    mul = functools.partial(jnp.dot, preferred_element_type=jnp.float32)
    return mul(ah, bh) + (mul(ah, bl) + mul(al, bh))


def width(part):
    return BOUNDS[part][1] - BOUNDS[part][0]


def term_kernel(part, z_ref, y_ref, c_ref, *refs):
    strips, outs, acc = refs[: -NY - 1], refs[-NY - 1 : -1], refs[-1]
    k = pl.program_id(0)
    product = dot3(c_ref[0], jnp.concatenate([e[0] for e in strips], axis=1))

    @pl.when(k == 0)
    def _():
        acc[...] = product

    @pl.when(k > 0)
    def _():
        acc[...] += product

    @pl.when(k == pl.num_programs(0) - 1)
    def _():
        shift = SHIFTS[part]
        label = (z_ref[0] + shift) % NZ
        for n, kz in enumerate(BITREV):
            z = ((label ^ kz) + NZ - shift) % NZ
            for ky, o_ref in enumerate(outs):
                row = pl.multiple_of((z * NY + (y_ref[0] ^ ky)) * SLAB, SLAB)
                o_ref[n] = acc[pl.ds(row, SLAB), :]


def term(z, y, coupling, earlier, part):
    n = 2 * width(part)
    at = BOUNDS[part][0] // STRIP
    strips = [half * (HALF // STRIP) + at + i for half in (0, 1) for i in range(width(part) // STRIP)]
    out = pl.BlockSpec((NZ, SLAB, n), lambda k, z, y: (0, 0, 0))
    return pl.pallas_call(
        functools.partial(term_kernel, part),
        grid_spec=pltpu.PrefetchScalarGridSpec(
            num_scalar_prefetch=2,
            grid=(4,),
            in_specs=[pl.BlockSpec((1, 512, 512), lambda k, z, y: (k, 0, 0))]
            + [pl.BlockSpec((1, 512, STRIP), lambda k, z, y, i=i: (k, 0, i)) for i in strips],
            out_specs=(out,) * NY,
            scratch_shapes=[pltpu.VMEM((512, n), jnp.float32)],
        ),
        out_shape=(jax.ShapeDtypeStruct((NZ, SLAB, n), jnp.float32),) * NY,
        compiler_params=pltpu.CompilerParams(vmem_limit_bytes=56 * 2**20),
        cost_estimate=pl.CostEstimate(
            flops=6 * 512 * 2048 * n, bytes_accessed=2**22 + 2**13 * n, transcendentals=0
        ),
        name="term",
    )(z, y, coupling, *[earlier] * len(strips))


def copy_in(source, target, sem):
    copy = pltpu.make_async_copy(source, target, sem)
    copy.start()
    return copy


def solve_kernel(n, y_ref, core_ref, inv_hbm, other_hbm, *refs):
    pieces, links, (o_ref, b, inv, link, sems) = refs[:-10], refs[-10:-5], refs[-5:]
    y, core = y_ref[0], core_ref[0]
    begun = [0]

    def begin(source, target):
        begun[0] += 1
        return copy_in(source, target, sems.at[begun[0] - 1])

    def block(k):
        at = pl.ds(k * n, n)
        copies = [begin(inv_hbm.at[k], inv.at[k])]
        if len(pieces) > 1:
            for p, (by, z, count) in zip(pieces, PLACES):
                copies.append(begin(p.at[:, :, at], b.at[k, pl.ds(z, count), (y + by) % NY]))
        else:
            for ky in range(NY):
                copies.append(begin(pieces[0].at[:, ky, :, at], b.at[k, :, y ^ ky]))
        return copies

    here = pl.ds(pl.multiple_of(core * 256, 128), 256)
    there = pl.ds(pl.multiple_of((1 - core) * 256, 128), 256)
    copies0, copies1 = block(0), block(1)
    for p, (by, z, count) in zip(links, PLACES):
        target = link.at[pl.ds(z, count), (y + by) % NY]
        copies1.append(begin(p.at[:, :, pl.ds(p.shape[2] - 256, 256)], target.at[:, :, here]))
    for i, by in enumerate((0, -1, 1, 2)):
        copies1.append(begin(other_hbm.at[i], link.at[:, (y + by + NY) % NY, :, there]))
    for copy in copies0:
        copy.wait()
    first = dot3(inv[0], b[0].reshape(512, n))
    o_ref[0] = first
    for copy in copies1:
        copy.wait()
    middle = b[1].reshape(512, n) - dot3(link[...].reshape(512, 512), first)
    o_ref[1] = dot3(inv[1], middle)


def solve(n, y, core, inverses, other, pieces, links):
    scalar, anywhere = pl.BlockSpec(memory_space=pltpu.SMEM), pl.BlockSpec(memory_space=pl.ANY)
    return pl.pallas_call(
        functools.partial(solve_kernel, n),
        in_specs=[scalar] * 2 + [anywhere] * (2 + len(pieces) + len(links)),
        out_specs=pl.BlockSpec(memory_space=pltpu.VMEM),
        scratch_shapes=[
            pltpu.VMEM((2, NZ, NY, SLAB, n), jnp.float32),
            pltpu.VMEM((2, 512, 512), jnp.float32),
            pltpu.VMEM((NZ, NY, SLAB, 512), jnp.float32),
            pltpu.SemaphoreType.DMA((21,)),
        ],
        out_shape=jax.ShapeDtypeStruct((2, 512, n), jnp.float32),
        compiler_params=pltpu.CompilerParams(vmem_limit_bytes=60 * 2**20),
        cost_estimate=pl.CostEstimate(
            flops=18 * 512 * 512 * n, bytes_accessed=6 * 2**20, transcendentals=0
        ),
        name="solve",
    )(y, core, inverses, other, *pieces, *links)


def columns(part, half):
    return slice(half * HALF + BOUNDS[part][0], half * HALF + BOUNDS[part][1])


def finish_kernel(chunk, core_ref, own, other, base, panel, *refs):
    solved, pending, sems = refs[-3:]
    core = core_ref[0]
    first, last = BOUNDS[chunk]
    places = ((own, core * HALF + first), (other, (1 - core) * HALF + first))
    places = [(ref, pl.ds(pl.multiple_of(at, 128), last - first)) for ref, at in places]
    copies = [copy_in(ref, solved.at[:, :, at], sems.at[i]) for i, (ref, at) in enumerate(places)]
    for half in (0, 1):
        pending[:, columns(chunk, half)] = base[:, half * (last - first) : (half + 1) * (last - first)]
    for ref, at in places:
        update = dot3(panel[0], ref[0]) + dot3(panel[1], ref[1])
        pending[:, at] = pending[:, at] - update
    if len(refs) > 3:
        for half in (0, 1):
            pending[:, columns(1 - chunk, half)] = refs[1][:, columns(1 - chunk, half)]
    for copy in copies:
        copy.wait()


def finish(chunk, core, own, other, base, panel, *before):
    whole, anywhere = pl.BlockSpec(memory_space=pltpu.VMEM), pl.BlockSpec(memory_space=pl.ANY)
    return pl.pallas_call(
        functools.partial(finish_kernel, chunk),
        in_specs=[pl.BlockSpec(memory_space=pltpu.SMEM)] + [whole] * 4 + [anywhere, whole][: len(before)],
        out_specs=(anywhere, whole),
        scratch_shapes=[pltpu.SemaphoreType.DMA((2,))],
        out_shape=(
            jax.ShapeDtypeStruct((2, 512, 2 * HALF), jnp.float32),
            jax.ShapeDtypeStruct((SLAB, 2 * HALF), jnp.float32),
        ),
        input_output_aliases={5: 0} if before else {},
        compiler_params=pltpu.CompilerParams(vmem_limit_bytes=24 * 2**20),
        cost_estimate=pl.CostEstimate(
            flops=24 * SLAB * 512 * (BOUNDS[chunk][1] - BOUNDS[chunk][0]), bytes_accessed=6 * 2**20, transcendentals=0
        ),
        name="finish",
    )(core, own, other, base, panel, *before)


def swap(x, axis, bit, shift=0):
    n = lax.axis_size(axis)
    return lax.ppermute(x, axis, [(i, (((i + shift) % n ^ bit) - shift) % n) for i in range(n)])


def after(x, *others):
    return lax.optimization_barrier((x, *others))[0]


def sum_y(slabs):
    near = slabs[0]
    for ky in (1, 3, 2):
        near = near + swap(slabs[ky], "y", ky)
    return near


def halve(s, bit, shift):
    n = s.shape[0] // 2
    return s[:n] + swap(s[n:], "z", bit, shift)


def sum_z(s, shift):
    for bit in (1, 2, 4):
        s = halve(s, bit, shift)
    return s[0]


def spread_x(v):
    others = [lax.ppermute(v, "x", [(NX - 1, i)]) for i in (2, 0, 1)]
    return jnp.where(lax.axis_index("x") == NX - 1, v, others[0] + others[1] + others[2])


def gather_z(v):
    return lax.all_to_all(jnp.broadcast_to(v, (NZ, *v.shape)), "z", 0, 0, tiled=True)


def gather_y(v):
    return [v] + [swap(v, "y", ky) for ky in range(1, NY)]


def step(x, axis, by):
    n = lax.axis_size(axis)
    return lax.ppermute(x, axis, [(i, (i + by) % n) for i in range(n)])


def gather_y_twice(v):
    up, down = step(v, "y", 1), step(v, "y", -1)
    h = NZ // 2
    return [v, up, down, step(up[:h], "y", 1), step(down[h:], "y", -1)]


def local(coupling, earlier, right_sides, panel_blocks, block_inverses):
    z, y, core = (lax.axis_index(a) for a in ("z", "y", "core"))
    coupling, earlier = coupling[0, 0, :, 0], earlier[:, 0]
    right, panel = right_sides[0, 0], panel_blocks[0, 0]
    is_first = core == 0
    z_id, y_id, core_id = (i.astype(jnp.int32).reshape(1) for i in (z, y, core))

    slabs_a = term(z_id, y_id, coupling, earlier, 0)
    slabs_b = term(z_id, y_id, after(coupling, *slabs_a), earlier, 1)
    near_a = halve(sum_y(slabs_a), 1, SHIFTS[0])
    near_b = sum_y([after(slabs_b[0], near_a), *slabs_b[1:]])
    total_a = halve(halve(near_a, 2, SHIFTS[0]), 4, SHIFTS[0])[0]
    total_b = sum_z(near_b, SHIFTS[1])
    def subtract(total, part):
        return jnp.concatenate([right[:, columns(part, half)] for half in (0, 1)], axis=1) - total

    def exchange(base, extra):
        n = base.shape[1] // 2
        kept = jnp.where(is_first, base[:, :n], base[:, n:])
        given = jnp.where(is_first, base[:, n:], base[:, :n])
        if extra is not None:
            given = jnp.concatenate([given, extra[:, 256:]], axis=1)
        came = swap(given, "core", 1)
        v = [jnp.where(is_first, came[:, :n], kept), jnp.where(is_first, kept, came[:, :n])]
        if extra is not None:
            v.append(jnp.where(is_first, extra[:, :256], came[:, n:]))
        return jnp.concatenate(v, axis=1)

    base_a, base_b = subtract(total_a, 0), subtract(total_b, 1)
    v_a = gather_z(spread_x(exchange(base_a, panel[0])))
    v_b = jnp.stack(gather_y(spread_x(exchange(base_b, None))))
    pieces_a = gather_y_twice(after(v_a, v_b))
    pieces_b = gather_z(v_b)

    part = jnp.concatenate([p[:, :, 2 * CUT :] for p in pieces_a]).reshape(NY, NZ, SLAB, 256)
    link = swap(part, "core", 1)
    own_a = solve(CUT, y_id, core_id, block_inverses, link, pieces_a, pieces_a)
    other_a = swap(own_a, "core", 1)
    own_b = solve(HALF - CUT, y_id, core_id, block_inverses, link, [pieces_b], pieces_a)
    other_b = swap(own_b, "core", 1)
    done_a = finish(0, core_id, own_a, other_a, base_a, panel)
    solved, pending = finish(1, core_id, own_b, other_b, base_b, panel, *done_a)
    return solved, pending[None, None]


def solution(mesh):
    inner = Mesh(mesh.devices.reshape(NZ, NY, NX, NCORE), ("z", "y", "x", "core"))
    row, col = ("z", "y"), ("x", "core")
    in_specs = (
        P(None, col, None, row, None, None),
        P(None, row, None, None),
        P(None, col, row, None),
        P(None, col, None, row, None),
        P(),
    )
    out_specs = (P(), P(None, col, row, None))
    return jax.shard_map(local, mesh=inner, in_specs=in_specs, out_specs=out_specs, check_vma=False)
```

```python
import functools

import jax
import jax.numpy as jnp
from jax import lax
from jax.experimental import pallas as pl
from jax.experimental.pallas import tpu as pltpu
from jax.sharding import Mesh
from jax.sharding import PartitionSpec as P

NZ, NY, NX, NCORE = 8, 4, 4, 2
SLAB = 16
HALF = 768
BITREV = (0, 4, 2, 6, 1, 5, 3, 7)
SHIFTS = (0, 1)
STRIP = 256
CUT = 512
BOUNDS = ((0, CUT), (CUT, HALF))
PLACES = ((0, 0, 8), (3, 0, 8), (1, 0, 8), (2, 0, 4), (2, 4, 4))


def split(x):
    high = x.astype(jnp.bfloat16)
    return high, (x - high.astype(jnp.float32)).astype(jnp.bfloat16)


def dot3(a, b):
    ah, al = split(a)
    bh, bl = split(b)
    mul = functools.partial(jnp.dot, preferred_element_type=jnp.float32)
    return mul(ah, bh) + (mul(ah, bl) + mul(al, bh))


def width(part):
    return BOUNDS[part][1] - BOUNDS[part][0]


def term_kernel(part, z_ref, y_ref, c_ref, *refs):
    strips, outs, acc = refs[: -NY - 1], refs[-NY - 1 : -1], refs[-1]
    k = pl.program_id(0)
    product = dot3(c_ref[0], jnp.concatenate([e[0] for e in strips], axis=1))

    @pl.when(k == 0)
    def _():
        acc[...] = product

    @pl.when(k > 0)
    def _():
        acc[...] += product

    @pl.when(k == pl.num_programs(0) - 1)
    def _():
        shift = SHIFTS[part]
        label = (z_ref[0] + shift) % NZ
        for n, kz in enumerate(BITREV):
            z = ((label ^ kz) + NZ - shift) % NZ
            for ky, o_ref in enumerate(outs):
                row = pl.multiple_of((z * NY + (y_ref[0] ^ ky)) * SLAB, SLAB)
                o_ref[n] = acc[pl.ds(row, SLAB), :]


def term(z, y, coupling, earlier, part):
    n = 2 * width(part)
    at = BOUNDS[part][0] // STRIP
    strips = [half * (HALF // STRIP) + at + i for half in (0, 1) for i in range(width(part) // STRIP)]
    out = pl.BlockSpec((NZ, SLAB, n), lambda k, z, y: (0, 0, 0))
    return pl.pallas_call(
        functools.partial(term_kernel, part),
        grid_spec=pltpu.PrefetchScalarGridSpec(
            num_scalar_prefetch=2,
            grid=(4,),
            in_specs=[pl.BlockSpec((1, 512, 512), lambda k, z, y: (k, 0, 0))]
            + [pl.BlockSpec((1, 512, STRIP), lambda k, z, y, i=i: (k, 0, i)) for i in strips],
            out_specs=(out,) * NY,
            scratch_shapes=[pltpu.VMEM((512, n), jnp.float32)],
        ),
        out_shape=(jax.ShapeDtypeStruct((NZ, SLAB, n), jnp.float32),) * NY,
        compiler_params=pltpu.CompilerParams(vmem_limit_bytes=56 * 2**20),
        cost_estimate=pl.CostEstimate(
            flops=6 * 512 * 2048 * n, bytes_accessed=2**22 + 2**13 * n, transcendentals=0
        ),
        name="term",
    )(z, y, coupling, *[earlier] * len(strips))


def copy_in(source, target, sem):
    copy = pltpu.make_async_copy(source, target, sem)
    copy.start()
    return copy


def solve_kernel(n, y_ref, core_ref, inv_hbm, other_hbm, *refs):
    pieces, links, (o_ref, b, inv, link, sems) = refs[:-10], refs[-10:-5], refs[-5:]
    y, core = y_ref[0], core_ref[0]
    begun = [0]

    def begin(source, target):
        begun[0] += 1
        return copy_in(source, target, sems.at[begun[0] - 1])

    def block(k):
        at = pl.ds(k * n, n)
        copies = [begin(inv_hbm.at[k], inv.at[k])]
        if len(pieces) > 1:
            for p, (by, z, count) in zip(pieces, PLACES):
                copies.append(begin(p.at[:, :, at], b.at[k, pl.ds(z, count), (y + by) % NY]))
        else:
            for ky in range(NY):
                copies.append(begin(pieces[0].at[:, ky, :, at], b.at[k, :, y ^ ky]))
        return copies

    here = pl.ds(pl.multiple_of(core * 256, 128), 256)
    there = pl.ds(pl.multiple_of((1 - core) * 256, 128), 256)
    copies0, copies1 = block(0), block(1)
    for p, (by, z, count) in zip(links, PLACES):
        target = link.at[pl.ds(z, count), (y + by) % NY]
        copies1.append(begin(p.at[:, :, pl.ds(p.shape[2] - 256, 256)], target.at[:, :, here]))
    for i, by in enumerate((0, -1, 1, 2)):
        copies1.append(begin(other_hbm.at[i], link.at[:, (y + by + NY) % NY, :, there]))
    for copy in copies0:
        copy.wait()
    first = dot3(inv[0], b[0].reshape(512, n))
    o_ref[0] = first
    for copy in copies1:
        copy.wait()
    middle = b[1].reshape(512, n) - dot3(link[...].reshape(512, 512), first)
    o_ref[1] = dot3(inv[1], middle)


def solve(n, y, core, inverses, other, pieces, links):
    scalar, anywhere = pl.BlockSpec(memory_space=pltpu.SMEM), pl.BlockSpec(memory_space=pl.ANY)
    return pl.pallas_call(
        functools.partial(solve_kernel, n),
        in_specs=[scalar] * 2 + [anywhere] * (2 + len(pieces) + len(links)),
        out_specs=pl.BlockSpec(memory_space=pltpu.VMEM),
        scratch_shapes=[
            pltpu.VMEM((2, NZ, NY, SLAB, n), jnp.float32),
            pltpu.VMEM((2, 512, 512), jnp.float32),
            pltpu.VMEM((NZ, NY, SLAB, 512), jnp.float32),
            pltpu.SemaphoreType.DMA((21,)),
        ],
        out_shape=jax.ShapeDtypeStruct((2, 512, n), jnp.float32),
        compiler_params=pltpu.CompilerParams(vmem_limit_bytes=60 * 2**20),
        cost_estimate=pl.CostEstimate(
            flops=18 * 512 * 512 * n, bytes_accessed=6 * 2**20, transcendentals=0
        ),
        name="solve",
    )(y, core, inverses, other, *pieces, *links)


def columns(part, half):
    return slice(half * HALF + BOUNDS[part][0], half * HALF + BOUNDS[part][1])


def finish_kernel(chunk, core_ref, own, other, base, panel, *refs):
    solved, pending, sems = refs[-3:]
    core = core_ref[0]
    first, last = BOUNDS[chunk]
    places = ((own, core * HALF + first), (other, (1 - core) * HALF + first))
    places = [(ref, pl.ds(pl.multiple_of(at, 128), last - first)) for ref, at in places]
    copies = [copy_in(ref, solved.at[:, :, at], sems.at[i]) for i, (ref, at) in enumerate(places)]
    for half in (0, 1):
        pending[:, columns(chunk, half)] = base[:, half * (last - first) : (half + 1) * (last - first)]
    for ref, at in places:
        update = dot3(panel[0], ref[0]) + dot3(panel[1], ref[1])
        pending[:, at] = pending[:, at] - update
    if len(refs) > 3:
        for half in (0, 1):
            pending[:, columns(1 - chunk, half)] = refs[1][:, columns(1 - chunk, half)]
    for copy in copies:
        copy.wait()


def finish(chunk, core, own, other, base, panel, *before):
    whole, anywhere = pl.BlockSpec(memory_space=pltpu.VMEM), pl.BlockSpec(memory_space=pl.ANY)
    return pl.pallas_call(
        functools.partial(finish_kernel, chunk),
        in_specs=[pl.BlockSpec(memory_space=pltpu.SMEM)] + [whole] * 4 + [anywhere, whole][: len(before)],
        out_specs=(anywhere, whole),
        scratch_shapes=[pltpu.SemaphoreType.DMA((2,))],
        out_shape=(
            jax.ShapeDtypeStruct((2, 512, 2 * HALF), jnp.float32),
            jax.ShapeDtypeStruct((SLAB, 2 * HALF), jnp.float32),
        ),
        input_output_aliases={5: 0} if before else {},
        compiler_params=pltpu.CompilerParams(vmem_limit_bytes=24 * 2**20),
        cost_estimate=pl.CostEstimate(
            flops=24 * SLAB * 512 * (BOUNDS[chunk][1] - BOUNDS[chunk][0]), bytes_accessed=6 * 2**20, transcendentals=0
        ),
        name="finish",
    )(core, own, other, base, panel, *before)


def swap(x, axis, bit, shift=0):
    n = lax.axis_size(axis)
    return lax.ppermute(x, axis, [(i, (((i + shift) % n ^ bit) - shift) % n) for i in range(n)])


def after(x, *others):
    return lax.optimization_barrier((x, *others))[0]


def sum_y(slabs):
    near = slabs[0]
    for ky in (1, 3, 2):
        near = near + swap(slabs[ky], "y", ky)
    return near


def halve(s, bit, shift):
    n = s.shape[0] // 2
    return s[:n] + swap(s[n:], "z", bit, shift)


def sum_z(s, shift):
    for bit in (1, 2, 4):
        s = halve(s, bit, shift)
    return s[0]


def spread_x(v):
    others = [lax.ppermute(v, "x", [(NX - 1, i)]) for i in (2, 0, 1)]
    return jnp.where(lax.axis_index("x") == NX - 1, v, others[0] + others[1] + others[2])


def gather_z(v):
    return lax.all_to_all(jnp.broadcast_to(v, (NZ, *v.shape)), "z", 0, 0, tiled=True)


def gather_y(v):
    came = {ky: swap(v, "y", ky) for ky in (1, 3, 2)}
    return [v] + [came[ky] for ky in range(1, NY)]


def step(x, axis, by):
    n = lax.axis_size(axis)
    return lax.ppermute(x, axis, [(i, (i + by) % n) for i in range(n)])


def gather_y_twice(v):
    up, down = step(v, "y", 1), step(v, "y", -1)
    h = NZ // 2
    return [v, up, down, step(up[:h], "y", 1), step(down[h:], "y", -1)]


def local(coupling, earlier, right_sides, panel_blocks, block_inverses):
    z, y, core = (lax.axis_index(a) for a in ("z", "y", "core"))
    coupling, earlier = coupling[0, 0, :, 0], earlier[:, 0]
    right, panel = right_sides[0, 0], panel_blocks[0, 0]
    is_first = core == 0
    z_id, y_id, core_id = (i.astype(jnp.int32).reshape(1) for i in (z, y, core))

    slabs_a = term(z_id, y_id, coupling, earlier, 0)
    slabs_b = term(z_id, y_id, after(coupling, *slabs_a), earlier, 1)
    near_a = halve(sum_y(slabs_a), 1, SHIFTS[0])
    near_b = sum_y([after(slabs_b[0], near_a), *slabs_b[1:]])
    total_a = halve(halve(near_a, 2, SHIFTS[0]), 4, SHIFTS[0])[0]
    total_b = sum_z(near_b, SHIFTS[1])
    def subtract(total, part):
        return jnp.concatenate([right[:, columns(part, half)] for half in (0, 1)], axis=1) - total

    def exchange(base, extra):
        n = base.shape[1] // 2
        kept = jnp.where(is_first, base[:, :n], base[:, n:])
        given = jnp.where(is_first, base[:, n:], base[:, :n])
        if extra is not None:
            given = jnp.concatenate([given, extra[:, 256:]], axis=1)
        came = swap(given, "core", 1)
        v = [jnp.where(is_first, came[:, :n], kept), jnp.where(is_first, kept, came[:, :n])]
        if extra is not None:
            v.append(jnp.where(is_first, extra[:, :256], came[:, n:]))
        return jnp.concatenate(v, axis=1)

    base_a, base_b = subtract(total_a, 0), subtract(total_b, 1)
    v_a = gather_z(spread_x(exchange(base_a, panel[0])))
    v_b = jnp.stack(gather_y(spread_x(exchange(base_b, None))))
    pieces_a = gather_y_twice(after(v_a, v_b))
    pieces_b = gather_z(v_b)

    part = jnp.concatenate([p[:, :, 2 * CUT :] for p in pieces_a]).reshape(NY, NZ, SLAB, 256)
    link = swap(part, "core", 1)
    own_a = solve(CUT, y_id, core_id, block_inverses, link, pieces_a, pieces_a)
    other_a = swap(own_a, "core", 1)
    own_b = solve(HALF - CUT, y_id, core_id, block_inverses, link, [pieces_b], pieces_a)
    other_b = swap(own_b, "core", 1)
    done_a = finish(0, core_id, own_a, other_a, base_a, panel)
    solved, pending = finish(1, core_id, own_b, other_b, base_b, panel, *done_a)
    return solved, pending[None, None]


def solution(mesh):
    inner = Mesh(mesh.devices.reshape(NZ, NY, NX, NCORE), ("z", "y", "x", "core"))
    row, col = ("z", "y"), ("x", "core")
    in_specs = (
        P(None, col, None, row, None, None),
        P(None, row, None, None),
        P(None, col, row, None),
        P(None, col, None, row, None),
        P(),
    )
    out_specs = (P(), P(None, col, row, None))
    return jax.shard_map(local, mesh=inner, in_specs=in_specs, out_specs=out_specs, check_vma=False)
```
